32 devices in a mesh: seq: 8 (over z, y), dp: 4 (over x, core).
Axes of the slice: x: 2, y: 2, z: 4, core: 2. Of those that a mesh axis runs over, the one named last changes fastest.
Arguments:
- queries: bfloat16 [4, 3072, 2048], P('dp', 'seq'), may hold values from -0.59765625 to 0.59765625
- keys: bfloat16 [4, 3072, 2048], P('dp', 'seq'), may hold values from -0.59765625 to 0.59765625
- values: bfloat16 [4, 3072, 2048], P('dp', 'seq'), may hold values from -6 to 6
- output_gradient: bfloat16 [4, 3072, 2048], P('dp', 'seq'), may hold values from -0.59765625 to 0.59765625
- document_lengths: int32 [4, 8], P('dp'), may hold values from 1 to 768, 3072 in all within a row
- cutoff_rows: int32 [4, 3072], P('dp', 'seq'), may hold values 0 or 1
- head_decay_rate: float32 [16], replicated, may hold values from 1.6276042e-05 to 0.04, as said below
Outputs:
- query_grad: bfloat16 [4, 3072, 2048], P('dp', 'seq')
- key_grad: bfloat16 [4, 3072, 2048], P('dp', 'seq')
- value_grad: bfloat16 [4, 3072, 2048], P('dp', 'seq')
- rate_grad: float32 [16], replicated
The draws below stay inside these ranges and needn't reach their ends.
Inputs may be any that keep to these rules, and one draw needn't show every extreme that they name: `head_decay_rate`: a positive rate for each head.
All inputs are finite; a program needn't handle non-finite values. No bound on the sum of `cutoff_rows` on one device may be relied on, other than what follows from the above.
Results may differ from the reference program's by a relative error of at most 0.0034.
Values sent between devices are 32-bit elements; how exact they have to be, the bound alone decides.
A program may use at most 192 MiB of HBM per device.

```python
import math
import jax
import jax.numpy as jnp
import numpy as np
from jax import lax

HEADS = 16
HEAD_DIM = 128
BLOCK_TOKENS = 384
DOCS = 8
SEQUENCE_LENGTH = 3072
ALL_TOKENS = 12288
N_SEQ = 8
N_DP = 4


def draw_head_decay_rate(key, part):
    pick_key, slow_key, fast_key = jax.random.split(key, 3)
    slow_share = 0.5
    chosen = jax.random.uniform(pick_key, (HEADS,), jnp.float32) < slow_share
    slow_rate = jnp.exp(jnp.log(0.05 / SEQUENCE_LENGTH) + jax.random.uniform(slow_key, (HEADS,), jnp.float32) * jnp.log(10.0))
    fast_rate = jax.random.uniform(fast_key, (HEADS,), jnp.float32, minval=0.02, maxval=0.04)
    return jnp.where(chosen, slow_rate, fast_rate).astype(jnp.float32)


def with_ends(array, rng, smallest, largest):
    shape = array.shape
    index_at = [jax.random.randint(jax.random.fold_in(rng, axis), (), 0, shape[axis]) for axis in range(len(shape))]
    array = array.at[tuple(index_at)].set(smallest)
    longest = shape.index(max(shape))
    index_at[longest] = (index_at[longest] + 1) % shape[longest]
    return array.at[tuple(index_at)].set(largest)


def block_levels(rng, shape, cuts, smallest, top_value):
    gain, own = 1.0, jax.random.fold_in(rng, 6)
    for dim, blocks in cuts:
        heights = jnp.exp(jax.random.uniform(jax.random.fold_in(own, dim), (blocks,), jnp.float32, smallest / len(cuts), top_value / len(cuts)))
        gain = gain * jnp.repeat(heights, shape[dim] // blocks).reshape([-1 if axis == dim else 1 for axis in range(len(shape))])
    return gain


def length_profile(number_of, total, reach, skew):
    weights = [(1 << 20) // math.isqrt(grade ** skew) + 1 for grade in range(2, number_of + 1)]
    spare, counts = total - reach - (number_of - 1), [1] * (number_of - 1)
    while spare > 0:
        movable = [i for i in range(number_of - 1) if counts[i] < reach]
        mass, remaining = sum([weights[i] for i in movable]), spare
        for i in movable:
            extra = min(reach - counts[i], max(1, remaining * weights[i] // mass), spare)
            counts[i] = counts[i] + extra
            spare = spare - extra
    return np.array([reach] + counts)


def ragged_sizes(key, count, total, most, slope):
    if count == 2:
        one = jax.random.randint(key, (), max(1, total - most), min(most, total - 1) + 1)
        return jnp.stack([one, total - one])
    sizes = jnp.asarray(length_profile(count, total, most, slope), jnp.int32)
    couples = (count - 1) // 2
    source_of, receiver = sizes[1:1 + 2 * couples:2], sizes[2:2 + 2 * couples:2]
    slack = jnp.minimum(source_of - 1, most - receiver)
    passed = jax.random.randint(jax.random.fold_in(key, 1), (couples,), 0, 1 << 20) % (slack + 1)
    sizes = sizes.at[1:1 + 2 * couples:2].set(source_of - passed).at[2:2 + 2 * couples:2].set(receiver + passed)
    return sizes[jax.random.permutation(jax.random.fold_in(key, 2), count)]


def bell_draw(rng, shape, scale, bound, cuts=(), kind=jnp.bfloat16):
    result = jax.random.normal(rng, shape, jnp.float32) * scale
    if len(cuts) > 0:
        result = block_levels(rng, shape, cuts, -0.22, 0.18) * result
    return jnp.clip(result, min=-bound, max=bound).astype(kind)


def setup_inputs(seed: int = 0) -> dict:
    arg_keys = jax.random.split(jax.random.key(seed), 8)
    return {
        "queries": bell_draw(arg_keys[0], (N_DP, SEQUENCE_LENGTH, HEADS * HEAD_DIM), 0.1, 0.59765625, ((0, 4), (1, 8))),
        "keys": bell_draw(arg_keys[1], (N_DP, SEQUENCE_LENGTH, HEADS * HEAD_DIM), 0.1, 0.59765625, ((0, 4), (1, 8))),
        "values": bell_draw(arg_keys[2], (N_DP, SEQUENCE_LENGTH, HEADS * HEAD_DIM), 1.0, 6.0, ((0, 4), (1, 8))),
        "output_gradient": bell_draw(arg_keys[3], (N_DP, SEQUENCE_LENGTH, HEADS * HEAD_DIM), 0.1, 0.59765625, ((0, 4), (1, 8))),
        "document_lengths": jax.vmap(lambda own: ragged_sizes(own, DOCS, SEQUENCE_LENGTH, SEQUENCE_LENGTH // 4, 2))(jax.random.split(arg_keys[4], N_DP)).reshape((N_DP, DOCS)).astype(jnp.int32),
        "cutoff_rows": with_ends((jax.random.randint(arg_keys[5], (N_DP, SEQUENCE_LENGTH), 0, 8 * BLOCK_TOKENS) < 1).astype(jnp.int32), jax.random.fold_in(arg_keys[5], 1), 0, 1),
        "head_decay_rate": draw_head_decay_rate(jax.random.fold_in(arg_keys[7], 71), 0),
    }


cutoff_logarithm = math.log(0.7)
exact_mode = lax.Precision.HIGHEST

def block_mask_list(head_decay_rate, cutoff_list, row_position, start_list):
    is_start = jnp.any(row_position[:, None] == start_list[None, :], axis=1)
    seg_local = jnp.cumsum(is_start.astype(jnp.int32))
    begin = lax.optimization_barrier(jnp.max(jnp.where(start_list[None, :] <= row_position[:, None], start_list[None, :], 0), axis=1))
    position = (row_position - begin).astype(jnp.float32)
    logarithm_step = cutoff_list.astype(jnp.float32)[:, None] * cutoff_logarithm - head_decay_rate[None, :]
    cum_log = jnp.cumsum(logarithm_step, axis=0)
    carry_in = jnp.where((seg_local == 0)[:, None], jnp.exp(cum_log), 0.0)
    carry_out = jnp.where((seg_local == seg_local[-1])[:, None], jnp.exp(cum_log[-1][None, :] - cum_log), 0.0)
    decay_all = jnp.where(seg_local[-1] == 0, jnp.exp(cum_log[-1]), 0.0)
    return (cum_log, seg_local, position, carry_in, carry_out, decay_all)

def weights_of(cum_log, seg_local):
    count = seg_local.shape[0]
    index = jnp.arange(count, dtype=jnp.int32)
    allowed = (seg_local[:, None] == seg_local[None, :]) & (index[:, None] >= index[None, :])
    spread = cum_log.T[:, :, None] - cum_log.T[:, None, :]
    return jnp.where(allowed[None], jnp.exp(jnp.where(allowed[None], spread, 0.0)), 0.0)

def block_summary(query_block, key_block, value_block, gradient_block, carry_in, carry_out):
    scaled_keys = carry_out[:, :, None] * key_block.astype(jnp.float32)
    scaled_queries = carry_in[:, :, None] * query_block.astype(jnp.float32)
    state_local = jnp.einsum('the,thf->hef', scaled_keys, value_block.astype(jnp.float32), precision=exact_mode)
    back_local = jnp.einsum('she,shf->hef', scaled_queries, gradient_block.astype(jnp.float32), precision=exact_mode)
    return (state_local, back_local)

def block_finish(query_block, key_block, value_block, gradient_block, mask_list, state_input, backward_input):
    cum_log, seg_local, position, carry_in, carry_out, decay_all = mask_list
    query_f = query_block.astype(jnp.float32)
    key_f = key_block.astype(jnp.float32)
    value_f = value_block.astype(jnp.float32)
    grad_f = gradient_block.astype(jnp.float32)
    weight = weights_of(cum_log, seg_local)
    scores = jnp.einsum('she,the->hst', query_f, key_f, precision=exact_mode)
    grad_scores = jnp.einsum('shf,thf->hst', grad_f, value_f, precision=exact_mode)
    attn_prob = (weight * scores).astype(jnp.bfloat16).astype(jnp.float32)
    grad_prob = (weight * grad_scores).astype(jnp.bfloat16).astype(jnp.float32)
    value_full = jnp.einsum('hst,shf->thf', attn_prob, grad_f, precision=exact_mode)
    value_full = value_full + carry_out[:, :, None] * jnp.einsum('the,hef->thf', key_f, backward_input, precision=exact_mode)
    query_full = jnp.einsum('hst,the->she', grad_prob, key_f, precision=exact_mode)
    query_full = query_full + carry_in[:, :, None] * jnp.einsum('shf,hef->she', grad_f, state_input, precision=exact_mode)
    key_full = jnp.einsum('hst,she->the', grad_prob, query_f, precision=exact_mode)
    key_full = key_full + carry_out[:, :, None] * jnp.einsum('thf,hef->the', value_f, backward_input, precision=exact_mode)
    inner_step = lax.optimization_barrier(jnp.sum(key_f * key_full, axis=2)) - lax.optimization_barrier(jnp.sum(query_f * query_full, axis=2))
    rate_part = lax.optimization_barrier(jnp.sum(position[:, None] * inner_step, axis=0))
    return (query_full.astype(jnp.bfloat16), key_full.astype(jnp.bfloat16), value_full.astype(jnp.bfloat16), rate_part)

def reference(queries, keys, values, output_gradient, document_lengths, cutoff_rows, head_decay_rate):
    block_shape = (N_DP, N_SEQ, BLOCK_TOKENS, HEADS, HEAD_DIM)
    query_every = queries.reshape(block_shape)
    key_every = keys.reshape(block_shape)
    value_every = values.reshape(block_shape)
    gradient_every = output_gradient.reshape(block_shape)
    cutoff_every = cutoff_rows.reshape(N_DP, N_SEQ, BLOCK_TOKENS)
    block_number = jnp.arange(N_SEQ, dtype=jnp.int32)
    local_rows = jnp.arange(BLOCK_TOKENS, dtype=jnp.int32)

    def single_sequence(item_list):
        query_sequence, key_sequence, value_sequence, gradient_sequence, length_list, cutoff_list = item_list
        start_list = (jnp.cumsum(length_list) - length_list).astype(jnp.int32)

        def block_digest(inner_step):
            block_piece, query_block, key_block, value_block, gradient_block, cutoff_block = inner_step
            row_position = (block_piece * BLOCK_TOKENS + local_rows).astype(jnp.int32)
            mask_list = block_mask_list(head_decay_rate, cutoff_block, row_position, start_list)
            state_local, back_local = block_summary(query_block, key_block, value_block, gradient_block, mask_list[3], mask_list[4])
            return (mask_list[5], state_local, back_local)
        decay_list, state_list, backward_list = lax.map(block_digest, (block_number, query_sequence, key_sequence, value_sequence, gradient_sequence, cutoff_list))
        zero_state = jnp.zeros((HEADS, HEAD_DIM, HEAD_DIM), jnp.float32)

        def forward(carry, inner_step):
            decay, state = inner_step
            return (decay[:, None, None] * carry + state, carry)

        def backward(carry, inner_step):
            decay, back = inner_step
            return (back + decay[:, None, None] * carry, carry)
        unused_a, state_input = lax.scan(forward, zero_state, (decay_list, state_list))
        unused_b, backward_input = lax.scan(backward, zero_state, (decay_list, backward_list), reverse=True)

        def finish_step(inner_step):
            block_piece, query_block, key_block, value_block, gradient_block, cutoff_block, state_block, backward_block = inner_step
            row_position = (block_piece * BLOCK_TOKENS + local_rows).astype(jnp.int32)
            mask_list = block_mask_list(head_decay_rate, cutoff_block, row_position, start_list)
            return block_finish(query_block, key_block, value_block, gradient_block, mask_list, state_block, backward_block)
        return lax.map(finish_step, (block_number, query_sequence, key_sequence, value_sequence, gradient_sequence, cutoff_list, state_input, backward_input))
    query_output, key_output, value_output, rate_pieces = lax.map(single_sequence, (query_every, key_every, value_every, gradient_every, document_lengths, cutoff_every))
    full_shape = (N_DP, SEQUENCE_LENGTH, HEADS * HEAD_DIM)
    rate_total = lax.optimization_barrier(jnp.sum(rate_pieces, axis=(0, 1)))
    rate_grad = head_decay_rate * rate_total / math.sqrt(ALL_TOKENS)
    return (query_output.reshape(full_shape), key_output.reshape(full_shape), value_output.reshape(full_shape), rate_grad)
```

```python
import functools
import math

import jax
import jax.numpy as jnp
from jax import lax
from jax.experimental import pallas as pl
from jax.experimental.pallas import tpu as pltpu
from jax.sharding import PartitionSpec as P

HEADS = 16
HEAD_DIM = 128


cutoff_logarithm = math.log(0.7)
state_mode = lax.Precision.HIGH


def carried_in(part, axis, combine, identity, reverse):
    count = lax.axis_size(axis)
    place = lax.axis_index(axis)
    ahead = count - 1 - place if reverse else place
    gathered = jax.tree.map(lambda a: lax.all_gather(a, axis), part)
    state = jax.tree.map(lambda a, e: jnp.zeros_like(a) + jnp.asarray(e, a.dtype), part, identity)

    def one(step, state):
        source = count - 1 - step if reverse else step
        return combine(
            state, jax.tree.map(lambda a: lax.dynamic_index_in_dim(a, source, 0, False), gathered)
        )

    return lax.fori_loop(0, ahead, one, state)


def block_mask_list(head_decay_rate, cutoff_list, row_position, start_list):
    is_start = jnp.any(row_position[:, None] == start_list[None, :], axis=1)
    seg_local = jnp.cumsum(is_start.astype(jnp.int32))
    begin = jnp.max(
        jnp.where(start_list[None, :] <= row_position[:, None], start_list[None, :], 0), axis=1
    )
    position = (row_position - begin).astype(jnp.float32)
    logarithm_step = (
        cutoff_list.astype(jnp.float32)[:, None] * cutoff_logarithm - head_decay_rate[None, :]
    )
    cum_log = jnp.cumsum(logarithm_step, axis=0)
    carry_in = jnp.where((seg_local == 0)[:, None], jnp.exp(cum_log), 0.0)
    carry_out = jnp.where(
        (seg_local == seg_local[-1])[:, None], jnp.exp(cum_log[-1][None, :] - cum_log), 0.0
    )
    decay_all = jnp.where(seg_local[-1] == 0, jnp.exp(cum_log[-1]), 0.0)
    return (cum_log, seg_local, position, carry_in, carry_out, decay_all)


def weights_of(cum_log, seg_local):
    count = seg_local.shape[0]
    index = jnp.arange(count, dtype=jnp.int32)
    allowed = (seg_local[:, None] == seg_local[None, :]) & (index[:, None] >= index[None, :])
    spread = cum_log.T[:, :, None] - cum_log.T[:, None, :]
    return jnp.where(allowed[None], jnp.exp(jnp.where(allowed[None], spread, 0.0)), 0.0)


def forward_combine(earlier, later):
    return (earlier[0] * later[0], later[0][:, None, None] * earlier[1] + later[1])


def backward_combine(earlier, later):
    return (later[0] * earlier[0], later[1] + later[0][:, None, None] * earlier[1])


def on_device(
    queries, keys, values, output_gradient, document_lengths, cutoff_rows, head_decay_rate
):
    row_count = queries.shape[1]
    query_block = queries.reshape(row_count, HEADS, HEAD_DIM)
    key_block = keys.reshape(row_count, HEADS, HEAD_DIM)
    value_block = values.reshape(row_count, HEADS, HEAD_DIM)
    gradient_block = output_gradient.reshape(row_count, HEADS, HEAD_DIM)
    block_piece = lax.axis_index("seq")
    row_position = block_piece * row_count + jnp.arange(row_count, dtype=jnp.int32)
    length_list = document_lengths[0]
    start_list = jnp.cumsum(length_list) - length_list
    cum_log, seg_local, position, carry_in, carry_out, decay_all = block_mask_list(
        head_decay_rate, cutoff_rows[0], row_position, start_list
    )
    key_f = key_block.astype(jnp.float32)
    value_f = value_block.astype(jnp.float32)
    grad_f = gradient_block.astype(jnp.float32)
    query_f = query_block.astype(jnp.float32)
    state_local = jnp.einsum(
        "the,thf->hef", carry_out[:, :, None] * key_f, value_f, precision=state_mode
    )
    back_local = jnp.einsum(
        "she,shf->hef", carry_in[:, :, None] * query_f, grad_f, precision=state_mode
    )
    identity = (jnp.ones_like(decay_all), jnp.zeros_like(state_local))
    state_input = carried_in((decay_all, state_local), "seq", forward_combine, identity, False)[1]
    backward_input = carried_in((decay_all, back_local), "seq", backward_combine, identity, True)[1]
    weight = weights_of(cum_log, seg_local)
    scores = jnp.einsum("she,the->hst", query_block, key_block, preferred_element_type=jnp.float32)
    grad_scores = jnp.einsum(
        "shf,thf->hst", gradient_block, value_block, preferred_element_type=jnp.float32
    )
    attn_prob = (weight * scores).astype(jnp.bfloat16)
    grad_prob = (weight * grad_scores).astype(jnp.bfloat16)
    value_full = jnp.einsum(
        "hst,shf->thf", attn_prob, gradient_block, preferred_element_type=jnp.float32
    )
    value_full = value_full + carry_out[:, :, None] * jnp.einsum(
        "the,hef->thf", key_f, backward_input, precision=state_mode
    )
    query_full = jnp.einsum(
        "hst,the->she", grad_prob, key_block, preferred_element_type=jnp.float32
    )
    query_full = query_full + carry_in[:, :, None] * jnp.einsum(
        "shf,hef->she", grad_f, state_input, precision=state_mode
    )
    key_full = jnp.einsum(
        "hst,she->the", grad_prob, query_block, preferred_element_type=jnp.float32
    )
    key_full = key_full + carry_out[:, :, None] * jnp.einsum(
        "thf,hef->the", value_f, backward_input, precision=state_mode
    )
    inner_step = jnp.sum(key_f * key_full, axis=2) - jnp.sum(query_f * query_full, axis=2)
    rate_part = jnp.sum(position[:, None] * inner_step, axis=0)
    rate_total = lax.psum(rate_part, ("seq", "dp"))
    token_total = row_count * lax.axis_size("seq") * lax.axis_size("dp")
    rate_grad = head_decay_rate * rate_total / math.sqrt(token_total)
    out_shape = (1, row_count, HEADS * HEAD_DIM)
    return (
        query_full.astype(jnp.bfloat16).reshape(out_shape),
        key_full.astype(jnp.bfloat16).reshape(out_shape),
        value_full.astype(jnp.bfloat16).reshape(out_shape),
        rate_grad,
    )


MESH_ID = pl.DeviceIdType.MESH
CHUNK_HEADS = 2
CHUNKS = HEADS // CHUNK_HEADS
MASKED = -1e30


def dot(a, b, contract):
    return lax.dot_general(
        a, b, ((contract[:1], contract[1:]), ((), ())), preferred_element_type=jnp.float32
    )


def halves(array):
    high = array.astype(jnp.bfloat16)
    return high, (array - high.astype(jnp.float32)).astype(jnp.bfloat16)


def near_kernel(
    lengths,
    rates,
    cutoffs,
    queries,
    keys,
    values,
    gradients,
    query_out,
    key_out,
    value_out,
    rate_out,
    spread,
    distance,
    log_in,
    log_out,
    place,
    decays,
    near_decays,
    states,
    from_pair,
    from_line,
    relayed,
    query_sum,
    key_sum,
    value_sum,
    rate_rows,
    rate_dp,
    rate_seq,
    pair_send,
    pair_recv,
    line_send,
    line_recv,
    relay_send,
    relay_recv,
    decay_send,
    decay_recv,
    dp_send,
    dp_recv,
    seq_send,
    seq_recv,
):
    n_seq, n_dp = lax.axis_size("seq"), lax.axis_size("dp")
    block, part = lax.axis_index("seq"), lax.axis_index("dp")
    rows = queries.shape[0]
    side = lax.rem(block, 2)
    pair = block + 1 - 2 * side
    is_first, is_last = block < 2, block >= n_seq - 2
    has_relay = jnp.where(side == 1, block, n_seq - 1 - block) >= 2
    gets_relay = jnp.where(side == 0, block, n_seq - 1 - block) >= 2

    barrier = pltpu.get_barrier_semaphore()
    for other in range(1, n_seq):
        pl.semaphore_signal(
            barrier,
            inc=1,
            device_id={"seq": lax.rem(block + other, n_seq)},
            device_id_type=MESH_ID,
        )
    for other in range(1, n_dp):
        pl.semaphore_signal(
            barrier, inc=1, device_id={"dp": lax.rem(part + other, n_dp)}, device_id_type=MESH_ID
        )

    first = block * rows
    starts, total = [], jnp.int32(0)
    for j in range(lengths.shape[1]):
        starts.append(total)
        total = total + lengths[0, j]

    def segment(local):
        count = jnp.zeros(local.shape, jnp.int32)
        for start in starts:
            count = count + jnp.where((start >= first) & (local + first >= start), 1, 0)
        return count

    row_of = lax.broadcasted_iota(jnp.int32, (rows, rows), 0)
    column_of = lax.broadcasted_iota(jnp.int32, (rows, rows), 1)
    cut_row = cutoffs[...].astype(jnp.float32)
    cut_all = jnp.broadcast_to(cut_row, (rows, rows))
    count_column = jnp.sum(jnp.where(column_of <= row_of, cut_all, 0.0), axis=1, keepdims=True)
    cut_column = jnp.sum(jnp.where(column_of == row_of, cut_all, 0.0), axis=1, keepdims=True)
    count_row = jnp.sum(jnp.where(row_of <= column_of, cut_column, 0.0), axis=0, keepdims=True)
    count_last = jnp.sum(cut_row, axis=1, keepdims=True)
    allowed = (segment(row_of) == segment(column_of)) & (row_of >= column_of)
    spread[...] = jnp.where(allowed, (count_column - count_row) * cutoff_logarithm, MASKED)
    distance[...] = (row_of - column_of).astype(jnp.float32)
    local = lax.broadcasted_iota(jnp.int32, (rows, HEAD_DIM), 0)
    last = jnp.full((rows, HEAD_DIM), rows - 1, jnp.int32)
    piece = segment(local)
    piece_last = segment(last)
    log_in[...] = jnp.where(piece == 0, count_column * cutoff_logarithm, MASKED)
    log_out[...] = jnp.where(
        piece == piece_last, (count_last - count_column) * cutoff_logarithm, MASKED
    )
    begin = jnp.zeros((rows, HEAD_DIM), jnp.int32)
    for start in starts:
        begin = jnp.maximum(begin, jnp.where(local + first >= start, start, 0))
    place[...] = (local + first - begin).astype(jnp.float32)
    log_all = jnp.where(piece_last[:1] == 0, count_last * cutoff_logarithm, MASKED)
    for h in range(HEADS):
        decays[h : h + 1, :] = jnp.exp(log_all - rates[h] * float(rows))

    @pl.when(is_first)
    def _():
        from_line[0] = jnp.zeros(from_line.shape[1:], jnp.float32)

    @pl.when(is_last)
    def _():
        from_line[1] = jnp.zeros(from_line.shape[1:], jnp.float32)

    @pl.when(block == 0)
    def _():
        near_decays[0] = jnp.zeros(near_decays.shape[1:], jnp.float32)

    @pl.when(block == n_seq - 1)
    def _():
        near_decays[1] = jnp.zeros(near_decays.shape[1:], jnp.float32)

    @pl.when(jnp.logical_not(gets_relay))
    def _():
        relayed[...] = jnp.zeros(relayed.shape, jnp.float32)

    def chunk_of(chunk):
        return pl.ds(pl.multiple_of(chunk * CHUNK_HEADS, CHUNK_HEADS), CHUNK_HEADS)

    def pair_copy(chunk):
        return pltpu.make_async_remote_copy(
            src_ref=states.at[side, chunk_of(chunk)],
            dst_ref=from_pair.at[chunk_of(chunk)],
            send_sem=pair_send.at[chunk],
            recv_sem=pair_recv.at[chunk],
            device_id={"seq": pair},
            device_id_type=MESH_ID,
        )

    def line_copy(way, chunk):
        target = jnp.minimum(block + 2, n_seq - 1) if way == 0 else jnp.maximum(block - 2, 0)
        return pltpu.make_async_remote_copy(
            src_ref=states.at[way, chunk_of(chunk)],
            dst_ref=from_line.at[way, chunk_of(chunk)],
            send_sem=line_send.at[way, chunk],
            recv_sem=line_recv.at[way, chunk],
            device_id={"seq": target},
            device_id_type=MESH_ID,
        )

    def relay_copy(chunk):
        return pltpu.make_async_remote_copy(
            src_ref=from_line.at[1 - side, chunk_of(chunk)],
            dst_ref=relayed.at[chunk_of(chunk)],
            send_sem=relay_send.at[chunk],
            recv_sem=relay_recv.at[chunk],
            device_id={"seq": pair},
            device_id_type=MESH_ID,
        )

    def decay_copy(way):
        target = jnp.minimum(block + 1, n_seq - 1) if way == 0 else jnp.maximum(block - 1, 0)
        return pltpu.make_async_remote_copy(
            src_ref=decays,
            dst_ref=near_decays.at[way],
            send_sem=decay_send.at[way],
            recv_sem=decay_recv.at[way],
            device_id={"seq": target},
            device_id_type=MESH_ID,
        )

    def head_columns(head):
        return pl.ds(pl.multiple_of(head * HEAD_DIM, HEAD_DIM), HEAD_DIM)

    def rows_since():
        return lax.broadcasted_iota(jnp.int32, (rows, HEAD_DIM), 0).astype(jnp.float32)

    def carry_in_of(head):
        return jnp.exp(log_in[...] - rates[head] * (rows_since() + 1.0))

    def carry_out_of(head):
        return jnp.exp(log_out[...] - rates[head] * (float(rows - 1) - rows_since()))

    pl.semaphore_wait(barrier, n_seq - 1 + n_dp - 1)

    not_end = jnp.logical_not(block == n_seq - 1)
    not_begin = jnp.logical_not(block == 0)

    @pl.when(not_end)
    def _():
        decay_copy(0).start()

    @pl.when(not_begin)
    def _():
        decay_copy(1).start()

    def own_states(chunk, carry):
        for inner in range(CHUNK_HEADS):
            head = chunk * CHUNK_HEADS + inner
            at = head_columns(head)
            high, low = halves(carry_out_of(head) * keys[:, at].astype(jnp.float32))
            value = values[:, at]
            states[0, head] = dot(high, value, (0, 0)) + dot(low, value, (0, 0))
            high, low = halves(carry_in_of(head) * queries[:, at].astype(jnp.float32))
            gradient = gradients[:, at]
            states[1, head] = dot(high, gradient, (0, 0)) + dot(low, gradient, (0, 0))
        pair_copy(chunk).start()

        @pl.when(jnp.logical_not(is_last))
        def _():
            line_copy(0, chunk).start()

        @pl.when(jnp.logical_not(is_first))
        def _():
            line_copy(1, chunk).start()

        return carry

    lax.fori_loop(0, CHUNKS, own_states, 0)

    def within(chunk, carry):
        for inner in range(CHUNK_HEADS):
            head = chunk * CHUNK_HEADS + inner
            at = head_columns(head)
            query, key = queries[:, at], keys[:, at]
            value, gradient = values[:, at], gradients[:, at]
            weight = jnp.exp(spread[...] - rates[head] * distance[...])
            attn_prob = (weight * dot(query, key, (1, 1))).astype(jnp.bfloat16)
            grad_prob = (weight * dot(gradient, value, (1, 1))).astype(jnp.bfloat16)
            value_sum[:, at] = dot(attn_prob, gradient, (0, 0))
            query_sum[:, at] = dot(grad_prob, key, (1, 0))
            key_sum[:, at] = dot(grad_prob, query, (0, 0))

        @pl.when(has_relay)
        def _():
            @pl.when(side == 1)
            def _():
                line_copy(0, chunk).wait_recv()

            @pl.when(side == 0)
            def _():
                line_copy(1, chunk).wait_recv()

            relay_copy(chunk).start()

        return carry

    lax.fori_loop(0, CHUNKS, within, 0)

    @pl.when(not_begin)
    def _():
        decay_copy(0).wait_recv()

    @pl.when(not_end)
    def _():
        decay_copy(1).wait_recv()

    def twice(array):
        return jnp.concatenate((array, array), axis=1)

    def across(chunk, carry):
        pair_copy(chunk).wait_recv()

        @pl.when((side == 0) & jnp.logical_not(is_first))
        def _():
            line_copy(0, chunk).wait_recv()

        @pl.when((side == 1) & jnp.logical_not(is_last))
        def _():
            line_copy(1, chunk).wait_recv()

        @pl.when(gets_relay)
        def _():
            relay_copy(chunk).wait_recv()

        for inner in range(CHUNK_HEADS):
            head = chunk * CHUNK_HEADS + inner
            at = head_columns(head)
            paired, passed = from_pair[head], relayed[head]
            before = jnp.where(side == 0, passed, paired)
            after = jnp.where(side == 0, paired, passed)
            state_in = before + near_decays[0, pl.ds(head, 1), :] * from_line[0, head]
            grad_in = after + near_decays[1, pl.ds(head, 1), :] * from_line[1, head]
            state_in = jnp.concatenate(halves(state_in), axis=1)
            high, low = halves(grad_in)
            grad_wide = jnp.concatenate((high, low), axis=1)
            grad_tall = jnp.concatenate((high, low), axis=0)
            query, key = queries[:, at], keys[:, at]
            carry_in, carry_out = carry_in_of(head), carry_out_of(head)
            query_full = query_sum[:, at] + carry_in * dot(
                twice(gradients[:, at]), state_in, (1, 1)
            )
            key_full = key_sum[:, at] + carry_out * dot(twice(values[:, at]), grad_wide, (1, 1))
            value_full = value_sum[:, at] + carry_out * dot(twice(key), grad_tall, (1, 0))
            query_out[:, at] = query_full.astype(jnp.bfloat16)
            key_out[:, at] = key_full.astype(jnp.bfloat16)
            value_out[:, at] = value_full.astype(jnp.bfloat16)
            inner_step = key.astype(jnp.float32) * key_full - query.astype(jnp.float32) * query_full
            rate_rows[pl.ds(head, 1), :] = jnp.sum(
                place[...] * inner_step, axis=0, keepdims=True
            )
        return carry

    lax.fori_loop(0, CHUNKS, across, 0)

    def dp_copy(other):
        return pltpu.make_async_remote_copy(
            src_ref=rate_rows,
            dst_ref=rate_dp.at[other],
            send_sem=dp_send.at[other],
            recv_sem=dp_recv.at[other],
            device_id={"dp": lax.rem(part + other, n_dp)},
            device_id_type=MESH_ID,
        )

    def seq_copy(other):
        return pltpu.make_async_remote_copy(
            src_ref=rate_seq.at[0],
            dst_ref=rate_seq.at[other],
            send_sem=seq_send.at[other],
            recv_sem=seq_recv.at[other],
            device_id={"seq": lax.rem(block + other, n_seq)},
            device_id_type=MESH_ID,
        )

    for other in range(1, n_dp):
        dp_copy(other).start()
    summed = rate_rows[...]
    for other in range(1, n_dp):
        dp_copy(other).wait_recv()
        summed = summed + rate_dp[other]
    rate_seq[0] = summed
    for other in range(1, n_seq):
        seq_copy(other).start()
    for other in range(1, n_seq):
        seq_copy(other).wait_recv()
        summed = summed + rate_seq[other]
    rate_out[...] = jnp.sum(summed, axis=1, keepdims=True)

    for other in range(1, n_dp):
        dp_copy(other).wait_send()
    for other in range(1, n_seq):
        seq_copy(other).wait_send()

    @pl.when(not_end)
    def _():
        decay_copy(0).wait_send()

    @pl.when(not_begin)
    def _():
        decay_copy(1).wait_send()

    def sent(chunk, carry):
        pair_copy(chunk).wait_send()

        @pl.when(jnp.logical_not(is_last))
        def _():
            line_copy(0, chunk).wait_send()

        @pl.when(jnp.logical_not(is_first))
        def _():
            line_copy(1, chunk).wait_send()

        @pl.when(has_relay)
        def _():
            relay_copy(chunk).wait_send()

        return carry

    lax.fori_loop(0, CHUNKS, sent, 0)


def on_device_near(
    queries, keys, values, output_gradient, document_lengths, cutoff_rows, head_decay_rate
):
    rows, width = queries.shape[1:]
    n_seq, n_dp = lax.axis_size("seq"), lax.axis_size("dp")
    vmem = pl.BlockSpec(memory_space=pltpu.VMEM)
    smem = pl.BlockSpec(memory_space=pltpu.SMEM)
    out = jax.ShapeDtypeStruct((rows, width), jnp.bfloat16)
    state = (HEADS, HEAD_DIM, HEAD_DIM)
    dma = pltpu.SemaphoreType.DMA
    query_grad, key_grad, value_grad, rate_total = pl.pallas_call(
        near_kernel,
        out_shape=(out, out, out, jax.ShapeDtypeStruct((HEADS, 1), jnp.float32)),
        in_specs=[smem, smem] + [vmem] * 5,
        out_specs=[vmem] * 4,
        scratch_shapes=[
            pltpu.VMEM((rows, rows), jnp.float32),
            pltpu.VMEM((rows, rows), jnp.float32),
            pltpu.VMEM((rows, HEAD_DIM), jnp.float32),
            pltpu.VMEM((rows, HEAD_DIM), jnp.float32),
            pltpu.VMEM((rows, HEAD_DIM), jnp.float32),
            pltpu.VMEM((HEADS, HEAD_DIM), jnp.float32),
            pltpu.VMEM((2, HEADS, HEAD_DIM), jnp.float32),
            pltpu.VMEM((2,) + state, jnp.float32),
            pltpu.VMEM(state, jnp.float32),
            pltpu.VMEM((2,) + state, jnp.float32),
            pltpu.VMEM(state, jnp.float32),
            pltpu.VMEM((rows, width), jnp.float32),
            pltpu.VMEM((rows, width), jnp.float32),
            pltpu.VMEM((rows, width), jnp.float32),
            pltpu.VMEM((HEADS, HEAD_DIM), jnp.float32),
            pltpu.VMEM((n_dp, HEADS, HEAD_DIM), jnp.float32),
            pltpu.VMEM((n_seq, HEADS, HEAD_DIM), jnp.float32),
            dma((CHUNKS,)),
            dma((CHUNKS,)),
            dma((2, CHUNKS)),
            dma((2, CHUNKS)),
            dma((CHUNKS,)),
            dma((CHUNKS,)),
            dma((2,)),
            dma((2,)),
            dma((n_dp,)),
            dma((n_dp,)),
            dma((n_seq,)),
            dma((n_seq,)),
        ],
        compiler_params=pltpu.CompilerParams(
            collective_id=0, has_side_effects=True, vmem_limit_bytes=48 * 1024 * 1024
        ),
    )(
        document_lengths,
        head_decay_rate,
        cutoff_rows,
        queries[0],
        keys[0],
        values[0],
        output_gradient[0],
    )
    token_total = rows * n_seq * n_dp
    rate_grad = head_decay_rate * rate_total[:, 0] / math.sqrt(token_total)
    return (query_grad[None], key_grad[None], value_grad[None], rate_grad)


def solution(mesh):
    in_specs = (
        P("dp", "seq", None),
        P("dp", "seq", None),
        P("dp", "seq", None),
        P("dp", "seq", None),
        P("dp", None),
        P("dp", "seq"),
        P(),
    )
    out_specs = (P("dp", "seq", None), P("dp", "seq", None), P("dp", "seq", None), P())
    near = mesh.shape["seq"] == 8
    return jax.shard_map(
        on_device_near if near else on_device, mesh=mesh, in_specs=in_specs, out_specs=out_specs, check_vma=False
    )
```

```python
import functools
import math

import jax
import jax.numpy as jnp
from jax import lax
from jax.experimental import pallas as pl
from jax.experimental.pallas import tpu as pltpu
from jax.sharding import PartitionSpec as P

HEADS = 16
HEAD_DIM = 128


cutoff_logarithm = math.log(0.7)
state_mode = lax.Precision.HIGH


def carried_in(part, axis, combine, identity, reverse):
    count = lax.axis_size(axis)
    place = lax.axis_index(axis)
    ahead = count - 1 - place if reverse else place
    gathered = jax.tree.map(lambda a: lax.all_gather(a, axis), part)
    state = jax.tree.map(lambda a, e: jnp.zeros_like(a) + jnp.asarray(e, a.dtype), part, identity)

    def one(step, state):
        source = count - 1 - step if reverse else step
        return combine(
            state, jax.tree.map(lambda a: lax.dynamic_index_in_dim(a, source, 0, False), gathered)
        )

    return lax.fori_loop(0, ahead, one, state)


def block_mask_list(head_decay_rate, cutoff_list, row_position, start_list):
    is_start = jnp.any(row_position[:, None] == start_list[None, :], axis=1)
    seg_local = jnp.cumsum(is_start.astype(jnp.int32))
    begin = jnp.max(
        jnp.where(start_list[None, :] <= row_position[:, None], start_list[None, :], 0), axis=1
    )
    position = (row_position - begin).astype(jnp.float32)
    logarithm_step = (
        cutoff_list.astype(jnp.float32)[:, None] * cutoff_logarithm - head_decay_rate[None, :]
    )
    cum_log = jnp.cumsum(logarithm_step, axis=0)
    carry_in = jnp.where((seg_local == 0)[:, None], jnp.exp(cum_log), 0.0)
    carry_out = jnp.where(
        (seg_local == seg_local[-1])[:, None], jnp.exp(cum_log[-1][None, :] - cum_log), 0.0
    )
    decay_all = jnp.where(seg_local[-1] == 0, jnp.exp(cum_log[-1]), 0.0)
    return (cum_log, seg_local, position, carry_in, carry_out, decay_all)


def weights_of(cum_log, seg_local):
    count = seg_local.shape[0]
    index = jnp.arange(count, dtype=jnp.int32)
    allowed = (seg_local[:, None] == seg_local[None, :]) & (index[:, None] >= index[None, :])
    spread = cum_log.T[:, :, None] - cum_log.T[:, None, :]
    return jnp.where(allowed[None], jnp.exp(jnp.where(allowed[None], spread, 0.0)), 0.0)


def forward_combine(earlier, later):
    return (earlier[0] * later[0], later[0][:, None, None] * earlier[1] + later[1])


def backward_combine(earlier, later):
    return (later[0] * earlier[0], later[1] + later[0][:, None, None] * earlier[1])


def on_device(
    queries, keys, values, output_gradient, document_lengths, cutoff_rows, head_decay_rate
):
    row_count = queries.shape[1]
    query_block = queries.reshape(row_count, HEADS, HEAD_DIM)
    key_block = keys.reshape(row_count, HEADS, HEAD_DIM)
    value_block = values.reshape(row_count, HEADS, HEAD_DIM)
    gradient_block = output_gradient.reshape(row_count, HEADS, HEAD_DIM)
    block_piece = lax.axis_index("seq")
    row_position = block_piece * row_count + jnp.arange(row_count, dtype=jnp.int32)
    length_list = document_lengths[0]
    start_list = jnp.cumsum(length_list) - length_list
    cum_log, seg_local, position, carry_in, carry_out, decay_all = block_mask_list(
        head_decay_rate, cutoff_rows[0], row_position, start_list
    )
    key_f = key_block.astype(jnp.float32)
    value_f = value_block.astype(jnp.float32)
    grad_f = gradient_block.astype(jnp.float32)
    query_f = query_block.astype(jnp.float32)
    state_local = jnp.einsum(
        "the,thf->hef", carry_out[:, :, None] * key_f, value_f, precision=state_mode
    )
    back_local = jnp.einsum(
        "she,shf->hef", carry_in[:, :, None] * query_f, grad_f, precision=state_mode
    )
    identity = (jnp.ones_like(decay_all), jnp.zeros_like(state_local))
    state_input = carried_in((decay_all, state_local), "seq", forward_combine, identity, False)[1]
    backward_input = carried_in((decay_all, back_local), "seq", backward_combine, identity, True)[1]
    weight = weights_of(cum_log, seg_local)
    scores = jnp.einsum("she,the->hst", query_block, key_block, preferred_element_type=jnp.float32)
    grad_scores = jnp.einsum(
        "shf,thf->hst", gradient_block, value_block, preferred_element_type=jnp.float32
    )
    attn_prob = (weight * scores).astype(jnp.bfloat16)
    grad_prob = (weight * grad_scores).astype(jnp.bfloat16)
    value_full = jnp.einsum(
        "hst,shf->thf", attn_prob, gradient_block, preferred_element_type=jnp.float32
    )
    value_full = value_full + carry_out[:, :, None] * jnp.einsum(
        "the,hef->thf", key_f, backward_input, precision=state_mode
    )
    query_full = jnp.einsum(
        "hst,the->she", grad_prob, key_block, preferred_element_type=jnp.float32
    )
    query_full = query_full + carry_in[:, :, None] * jnp.einsum(
        "shf,hef->she", grad_f, state_input, precision=state_mode
    )
    key_full = jnp.einsum(
        "hst,she->the", grad_prob, query_block, preferred_element_type=jnp.float32
    )
    key_full = key_full + carry_out[:, :, None] * jnp.einsum(
        "thf,hef->the", value_f, backward_input, precision=state_mode
    )
    inner_step = jnp.sum(key_f * key_full, axis=2) - jnp.sum(query_f * query_full, axis=2)
    rate_part = jnp.sum(position[:, None] * inner_step, axis=0)
    rate_total = lax.psum(rate_part, ("seq", "dp"))
    token_total = row_count * lax.axis_size("seq") * lax.axis_size("dp")
    rate_grad = head_decay_rate * rate_total / math.sqrt(token_total)
    out_shape = (1, row_count, HEADS * HEAD_DIM)
    return (
        query_full.astype(jnp.bfloat16).reshape(out_shape),
        key_full.astype(jnp.bfloat16).reshape(out_shape),
        value_full.astype(jnp.bfloat16).reshape(out_shape),
        rate_grad,
    )


MESH_ID = pl.DeviceIdType.MESH
CHUNK_HEADS = 2
CHUNKS = HEADS // CHUNK_HEADS
MASKED = -1e30


def dot(a, b, contract):
    return lax.dot_general(
        a, b, ((contract[:1], contract[1:]), ((), ())), preferred_element_type=jnp.float32
    )


def halves(array):
    high = array.astype(jnp.bfloat16)
    return high, (array - high.astype(jnp.float32)).astype(jnp.bfloat16)


def near_kernel(
    lengths_far,
    rates_far,
    cutoffs_far,
    queries_far,
    keys_far,
    values_far,
    gradients_far,
    query_out,
    key_out,
    value_out,
    rate_out,
    lengths,
    rates,
    cutoffs,
    queries,
    keys,
    values,
    gradients,
    spread,
    distance,
    log_in,
    log_out,
    place,
    decays,
    near_decays,
    states,
    from_pair,
    from_line,
    relayed,
    query_sum,
    key_sum,
    value_sum,
    rate_rows,
    rate_dp,
    rate_seq,
    loaded,
    pair_send,
    pair_recv,
    line_send,
    line_recv,
    relay_send,
    relay_recv,
    decay_send,
    decay_recv,
    dp_send,
    dp_recv,
    seq_send,
    seq_recv,
):
    n_seq, n_dp = lax.axis_size("seq"), lax.axis_size("dp")
    block, part = lax.axis_index("seq"), lax.axis_index("dp")
    rows = queries.shape[0]
    side = lax.rem(block, 2)
    pair = block + 1 - 2 * side
    is_first, is_last = block < 2, block >= n_seq - 2
    has_relay = jnp.where(side == 1, block, n_seq - 1 - block) >= 2
    gets_relay = jnp.where(side == 0, block, n_seq - 1 - block) >= 2

    loads = [
        pltpu.make_async_copy(far, near, loaded.at[i])
        for i, (far, near) in enumerate(
            (
                (lengths_far, lengths),
                (cutoffs_far, cutoffs),
                (rates_far, rates),
                (keys_far.at[0], keys),
                (values_far.at[0], values),
                (queries_far.at[0], queries),
                (gradients_far.at[0], gradients),
            )
        )
    ]
    for load in loads:
        load.start()

    barrier = pltpu.get_barrier_semaphore()
    for other in range(1, n_seq):
        pl.semaphore_signal(
            barrier,
            inc=1,
            device_id={"seq": lax.rem(block + other, n_seq)},
            device_id_type=MESH_ID,
        )
    for other in range(1, n_dp):
        pl.semaphore_signal(
            barrier, inc=1, device_id={"dp": lax.rem(part + other, n_dp)}, device_id_type=MESH_ID
        )

    for load in loads[:3]:
        load.wait()

    first = block * rows
    starts, total = [], jnp.int32(0)
    for j in range(lengths.shape[1]):
        starts.append(total)
        total = total + lengths[0, j]

    def segment(local):
        count = jnp.zeros(local.shape, jnp.int32)
        for start in starts:
            count = count + jnp.where((start >= first) & (local + first >= start), 1, 0)
        return count

    row_of = lax.broadcasted_iota(jnp.int32, (rows, rows), 0)
    column_of = lax.broadcasted_iota(jnp.int32, (rows, rows), 1)
    cut_row = cutoffs[...].astype(jnp.float32)
    cut_all = jnp.broadcast_to(cut_row, (rows, rows))
    count_column = jnp.sum(jnp.where(column_of <= row_of, cut_all, 0.0), axis=1, keepdims=True)
    cut_column = jnp.sum(jnp.where(column_of == row_of, cut_all, 0.0), axis=1, keepdims=True)
    count_row = jnp.sum(jnp.where(row_of <= column_of, cut_column, 0.0), axis=0, keepdims=True)
    count_last = jnp.sum(cut_row, axis=1, keepdims=True)
    local = lax.broadcasted_iota(jnp.int32, (rows, HEAD_DIM), 0)
    last = jnp.full((rows, HEAD_DIM), rows - 1, jnp.int32)
    piece = segment(local)
    piece_last = segment(last)
    log_in[...] = jnp.where(piece == 0, count_column * cutoff_logarithm, MASKED)
    log_out[...] = jnp.where(
        piece == piece_last, (count_last - count_column) * cutoff_logarithm, MASKED
    )
    log_all = jnp.where(piece_last[:1] == 0, count_last * cutoff_logarithm, MASKED)
    for h in range(HEADS):
        decays[h : h + 1, :] = jnp.exp(log_all - rates[h] * float(rows))

    @pl.when(is_first)
    def _():
        from_line[0] = jnp.zeros(from_line.shape[1:], jnp.float32)

    @pl.when(is_last)
    def _():
        from_line[1] = jnp.zeros(from_line.shape[1:], jnp.float32)

    @pl.when(block == 0)
    def _():
        near_decays[0] = jnp.zeros(near_decays.shape[1:], jnp.float32)

    @pl.when(block == n_seq - 1)
    def _():
        near_decays[1] = jnp.zeros(near_decays.shape[1:], jnp.float32)

    @pl.when(jnp.logical_not(gets_relay))
    def _():
        relayed[...] = jnp.zeros(relayed.shape, jnp.float32)

    def chunk_of(chunk):
        return pl.ds(pl.multiple_of(chunk * CHUNK_HEADS, CHUNK_HEADS), CHUNK_HEADS)

    def pair_copy(chunk):
        return pltpu.make_async_remote_copy(
            src_ref=states.at[side, chunk_of(chunk)],
            dst_ref=from_pair.at[chunk_of(chunk)],
            send_sem=pair_send.at[chunk],
            recv_sem=pair_recv.at[chunk],
            device_id={"seq": pair},
            device_id_type=MESH_ID,
        )

    def line_copy(way, chunk):
        target = jnp.minimum(block + 2, n_seq - 1) if way == 0 else jnp.maximum(block - 2, 0)
        return pltpu.make_async_remote_copy(
            src_ref=states.at[way, chunk_of(chunk)],
            dst_ref=from_line.at[way, chunk_of(chunk)],
            send_sem=line_send.at[way, chunk],
            recv_sem=line_recv.at[way, chunk],
            device_id={"seq": target},
            device_id_type=MESH_ID,
        )

    def relay_copy(chunk):
        return pltpu.make_async_remote_copy(
            src_ref=from_line.at[1 - side, chunk_of(chunk)],
            dst_ref=relayed.at[chunk_of(chunk)],
            send_sem=relay_send.at[chunk],
            recv_sem=relay_recv.at[chunk],
            device_id={"seq": pair},
            device_id_type=MESH_ID,
        )

    def decay_copy(way):
        target = jnp.minimum(block + 1, n_seq - 1) if way == 0 else jnp.maximum(block - 1, 0)
        return pltpu.make_async_remote_copy(
            src_ref=decays,
            dst_ref=near_decays.at[way],
            send_sem=decay_send.at[way],
            recv_sem=decay_recv.at[way],
            device_id={"seq": target},
            device_id_type=MESH_ID,
        )

    def head_columns(head):
        return pl.ds(pl.multiple_of(head * HEAD_DIM, HEAD_DIM), HEAD_DIM)

    def rows_since():
        return lax.broadcasted_iota(jnp.int32, (rows, HEAD_DIM), 0).astype(jnp.float32)

    def carry_in_of(head):
        return jnp.exp(log_in[...] - rates[head] * (rows_since() + 1.0))

    def carry_out_of(head):
        return jnp.exp(log_out[...] - rates[head] * (float(rows - 1) - rows_since()))

    pl.semaphore_wait(barrier, n_seq - 1 + n_dp - 1)

    not_end = jnp.logical_not(block == n_seq - 1)
    not_begin = jnp.logical_not(block == 0)

    @pl.when(not_end)
    def _():
        decay_copy(0).start()

    @pl.when(not_begin)
    def _():
        decay_copy(1).start()

    def own_states(chunk, carry):
        for inner in range(CHUNK_HEADS):
            head = chunk * CHUNK_HEADS + inner
            at = head_columns(head)
            high, low = halves(carry_out_of(head) * keys[:, at].astype(jnp.float32))
            value = values[:, at]
            states[0, head] = dot(high, value, (0, 0)) + dot(low, value, (0, 0))
            high, low = halves(carry_in_of(head) * queries[:, at].astype(jnp.float32))
            gradient = gradients[:, at]
            states[1, head] = dot(high, gradient, (0, 0)) + dot(low, gradient, (0, 0))
        pair_copy(chunk).start()

        @pl.when(jnp.logical_not(is_last))
        def _():
            line_copy(0, chunk).start()

        @pl.when(jnp.logical_not(is_first))
        def _():
            line_copy(1, chunk).start()

        return carry

    for load in loads[3:]:
        load.wait()
    lax.fori_loop(0, CHUNKS, own_states, 0)

    piece_row = segment(lax.broadcasted_iota(jnp.int32, (1, rows), 1))
    allowed = (piece[:, :1] == piece_row) & (row_of >= column_of)
    spread[...] = jnp.where(allowed, (count_column - count_row) * cutoff_logarithm, MASKED)
    distance[...] = (row_of - column_of).astype(jnp.float32)
    begin = jnp.zeros((rows, HEAD_DIM), jnp.int32)
    for start in starts:
        begin = jnp.maximum(begin, jnp.where(local + first >= start, start, 0))
    place[...] = (local + first - begin).astype(jnp.float32)

    def within(chunk, carry):
        for inner in range(CHUNK_HEADS):
            head = chunk * CHUNK_HEADS + inner
            at = head_columns(head)
            for step, (low, high) in enumerate(((0, rows - HEAD_DIM), (rows - HEAD_DIM, rows))):
                here, upto = slice(low, high), slice(0, high)
                query, key = queries[here, at], keys[upto, at]
                value, gradient = values[upto, at], gradients[here, at]
                weight = jnp.exp(spread[here, upto] - rates[head] * distance[here, upto])
                attn_prob = (weight * dot(query, key, (1, 1))).astype(jnp.bfloat16)
                grad_prob = (weight * dot(gradient, value, (1, 1))).astype(jnp.bfloat16)
                query_sum[here, at] = dot(grad_prob, key, (1, 0))
                value_part = dot(attn_prob, gradient, (0, 0))
                key_part = dot(grad_prob, query, (0, 0))
                if step == 0:
                    value_sum[upto, at] = value_part
                    key_sum[upto, at] = key_part
                else:
                    value_sum[:low, at] += value_part[:low]
                    key_sum[:low, at] += key_part[:low]
                    value_sum[low:, at] = value_part[low:]
                    key_sum[low:, at] = key_part[low:]

        @pl.when(has_relay)
        def _():
            @pl.when(side == 1)
            def _():
                line_copy(0, chunk).wait_recv()

            @pl.when(side == 0)
            def _():
                line_copy(1, chunk).wait_recv()

            relay_copy(chunk).start()

        return carry

    lax.fori_loop(0, CHUNKS, within, 0)

    @pl.when(not_begin)
    def _():
        decay_copy(0).wait_recv()

    @pl.when(not_end)
    def _():
        decay_copy(1).wait_recv()

    def twice(array):
        return jnp.concatenate((array, array), axis=1)

    def across(chunk, carry):
        pair_copy(chunk).wait_recv()

        @pl.when((side == 0) & jnp.logical_not(is_first))
        def _():
            line_copy(0, chunk).wait_recv()

        @pl.when((side == 1) & jnp.logical_not(is_last))
        def _():
            line_copy(1, chunk).wait_recv()

        @pl.when(gets_relay)
        def _():
            relay_copy(chunk).wait_recv()

        for inner in range(CHUNK_HEADS):
            head = chunk * CHUNK_HEADS + inner
            at = head_columns(head)
            paired, passed = from_pair[head], relayed[head]
            before = jnp.where(side == 0, passed, paired)
            after = jnp.where(side == 0, paired, passed)
            state_in = before + near_decays[0, pl.ds(head, 1), :] * from_line[0, head]
            grad_in = after + near_decays[1, pl.ds(head, 1), :] * from_line[1, head]
            state_in = jnp.concatenate(halves(state_in), axis=1)
            high, low = halves(grad_in)
            grad_wide = jnp.concatenate((high, low), axis=1)
            grad_tall = jnp.concatenate((high, low), axis=0)
            query, key = queries[:, at], keys[:, at]
            carry_in, carry_out = carry_in_of(head), carry_out_of(head)
            query_full = query_sum[:, at] + carry_in * dot(
                twice(gradients[:, at]), state_in, (1, 1)
            )
            key_full = key_sum[:, at] + carry_out * dot(twice(values[:, at]), grad_wide, (1, 1))
            value_full = value_sum[:, at] + carry_out * dot(twice(key), grad_tall, (1, 0))
            query_out[:, at] = query_full.astype(jnp.bfloat16)
            key_out[:, at] = key_full.astype(jnp.bfloat16)
            value_out[:, at] = value_full.astype(jnp.bfloat16)
            inner_step = key.astype(jnp.float32) * key_full - query.astype(jnp.float32) * query_full
            rate_rows[pl.ds(head, 1), :] = jnp.sum(
                place[...] * inner_step, axis=0, keepdims=True
            )
        return carry

    lax.fori_loop(0, CHUNKS, across, 0)

    def dp_copy(other):
        return pltpu.make_async_remote_copy(
            src_ref=rate_rows,
            dst_ref=rate_dp.at[other],
            send_sem=dp_send.at[other],
            recv_sem=dp_recv.at[other],
            device_id={"dp": lax.rem(part + other, n_dp)},
            device_id_type=MESH_ID,
        )

    def seq_copy(other):
        return pltpu.make_async_remote_copy(
            src_ref=rate_seq.at[0],
            dst_ref=rate_seq.at[other],
            send_sem=seq_send.at[other],
            recv_sem=seq_recv.at[other],
            device_id={"seq": lax.rem(block + other, n_seq)},
            device_id_type=MESH_ID,
        )

    for other in range(1, n_dp):
        dp_copy(other).start()
    summed = rate_rows[...]
    for other in range(1, n_dp):
        dp_copy(other).wait_recv()
        summed = summed + rate_dp[other]
    rate_seq[0] = summed
    for other in range(1, n_seq):
        seq_copy(other).start()
    for other in range(1, n_seq):
        seq_copy(other).wait_recv()
        summed = summed + rate_seq[other]
    scale = 1.0 / math.sqrt(rows * n_seq * n_dp)
    lane = lax.broadcasted_iota(jnp.int32, (1, HEAD_DIM), 1)
    summed = jnp.sum(summed, axis=1, keepdims=True) * scale
    result = jnp.zeros((1, HEAD_DIM), jnp.float32)
    for h in range(HEADS):
        result = jnp.where(lane == h, rates[h] * summed[h : h + 1], result)
    rate_out[...] = result[:, :HEADS]

    for other in range(1, n_dp):
        dp_copy(other).wait_send()
    for other in range(1, n_seq):
        seq_copy(other).wait_send()

    @pl.when(not_end)
    def _():
        decay_copy(0).wait_send()

    @pl.when(not_begin)
    def _():
        decay_copy(1).wait_send()

    def sent(chunk, carry):
        pair_copy(chunk).wait_send()

        @pl.when(jnp.logical_not(is_last))
        def _():
            line_copy(0, chunk).wait_send()

        @pl.when(jnp.logical_not(is_first))
        def _():
            line_copy(1, chunk).wait_send()

        @pl.when(has_relay)
        def _():
            relay_copy(chunk).wait_send()

        return carry

    lax.fori_loop(0, CHUNKS, sent, 0)


def finish_kernel(*refs):
    count = (len(refs) - 1) // 2
    copies = [
        pltpu.make_async_copy(refs[i], refs[count + i], refs[-1].at[i]) for i in range(count)
    ]
    for copy in copies:
        copy.start()
    for copy in copies:
        copy.wait()


def on_device_near(
    queries, keys, values, output_gradient, document_lengths, cutoff_rows, head_decay_rate
):
    rows, width = queries.shape[1:]
    n_seq, n_dp = lax.axis_size("seq"), lax.axis_size("dp")
    vmem = pl.BlockSpec(memory_space=pltpu.VMEM)
    hbm = pl.BlockSpec(memory_space=pltpu.HBM)
    anywhere = pl.BlockSpec(memory_space=pl.ANY)
    out = jax.ShapeDtypeStruct((rows, width), jnp.bfloat16)
    state = (HEADS, HEAD_DIM, HEAD_DIM)
    dma = pltpu.SemaphoreType.DMA
    near = pltpu.VMEM((rows, width), jnp.bfloat16)
    results = pl.pallas_call(
        near_kernel,
        out_shape=(out, out, out, jax.ShapeDtypeStruct((1, HEADS), jnp.float32)),
        in_specs=[hbm] * 7,
        out_specs=[vmem] * 4,
        scratch_shapes=[
            pltpu.SMEM(document_lengths.shape, jnp.int32),
            pltpu.SMEM(head_decay_rate.shape, jnp.float32),
            pltpu.VMEM(cutoff_rows.shape, jnp.int32),
            near,
            near,
            near,
            near,
            pltpu.VMEM((rows, rows), jnp.float32),
            pltpu.VMEM((rows, rows), jnp.float32),
            pltpu.VMEM((rows, HEAD_DIM), jnp.float32),
            pltpu.VMEM((rows, HEAD_DIM), jnp.float32),
            pltpu.VMEM((rows, HEAD_DIM), jnp.float32),
            pltpu.VMEM((HEADS, HEAD_DIM), jnp.float32),
            pltpu.VMEM((2, HEADS, HEAD_DIM), jnp.float32),
            pltpu.VMEM((2,) + state, jnp.float32),
            pltpu.VMEM(state, jnp.float32),
            pltpu.VMEM((2,) + state, jnp.float32),
            pltpu.VMEM(state, jnp.float32),
            pltpu.VMEM((rows, width), jnp.float32),
            pltpu.VMEM((rows, width), jnp.float32),
            pltpu.VMEM((rows, width), jnp.float32),
            pltpu.VMEM((HEADS, HEAD_DIM), jnp.float32),
            pltpu.VMEM((n_dp, HEADS, HEAD_DIM), jnp.float32),
            pltpu.VMEM((n_seq, HEADS, HEAD_DIM), jnp.float32),
            dma((7,)),
            dma((CHUNKS,)),
            dma((CHUNKS,)),
            dma((2, CHUNKS)),
            dma((2, CHUNKS)),
            dma((CHUNKS,)),
            dma((CHUNKS,)),
            dma((2,)),
            dma((2,)),
            dma((n_dp,)),
            dma((n_dp,)),
            dma((n_seq,)),
            dma((n_seq,)),
        ],
        compiler_params=pltpu.CompilerParams(
            collective_id=0, has_side_effects=True, vmem_limit_bytes=48 * 1024 * 1024
        ),
    )(
        document_lengths,
        head_decay_rate,
        cutoff_rows,
        queries,
        keys,
        values,
        output_gradient,
    )
    query_grad, key_grad, value_grad, rate_grad = pl.pallas_call(
        finish_kernel,
        out_shape=tuple(jax.ShapeDtypeStruct(a.shape, a.dtype) for a in results),
        in_specs=[anywhere] * 4,
        out_specs=[anywhere] * 4,
        scratch_shapes=[dma((4,))],
    )(*results)
    return (query_grad[None], key_grad[None], value_grad[None], rate_grad[0])


def solution(mesh):
    in_specs = (
        P("dp", "seq", None),
        P("dp", "seq", None),
        P("dp", "seq", None),
        P("dp", "seq", None),
        P("dp", None),
        P("dp", "seq"),
        P(),
    )
    out_specs = (P("dp", "seq", None), P("dp", "seq", None), P("dp", "seq", None), P())
    near = mesh.shape["seq"] == 8
    return jax.shard_map(
        on_device_near if near else on_device, mesh=mesh, in_specs=in_specs, out_specs=out_specs, check_vma=False
    )
```

```python
import functools
import math

import jax
import jax.numpy as jnp
from jax import lax
from jax.experimental import pallas as pl
from jax.experimental.pallas import tpu as pltpu
from jax.sharding import PartitionSpec as P

HEADS = 16
HEAD_DIM = 128


cutoff_logarithm = math.log(0.7)
state_mode = lax.Precision.HIGH


def carried_in(part, axis, combine, identity, reverse):
    count = lax.axis_size(axis)
    place = lax.axis_index(axis)
    ahead = count - 1 - place if reverse else place
    gathered = jax.tree.map(lambda a: lax.all_gather(a, axis), part)
    state = jax.tree.map(lambda a, e: jnp.zeros_like(a) + jnp.asarray(e, a.dtype), part, identity)

    def one(step, state):
        source = count - 1 - step if reverse else step
        return combine(
            state, jax.tree.map(lambda a: lax.dynamic_index_in_dim(a, source, 0, False), gathered)
        )

    return lax.fori_loop(0, ahead, one, state)


def block_mask_list(head_decay_rate, cutoff_list, row_position, start_list):
    is_start = jnp.any(row_position[:, None] == start_list[None, :], axis=1)
    seg_local = jnp.cumsum(is_start.astype(jnp.int32))
    begin = jnp.max(
        jnp.where(start_list[None, :] <= row_position[:, None], start_list[None, :], 0), axis=1
    )
    position = (row_position - begin).astype(jnp.float32)
    logarithm_step = (
        cutoff_list.astype(jnp.float32)[:, None] * cutoff_logarithm - head_decay_rate[None, :]
    )
    cum_log = jnp.cumsum(logarithm_step, axis=0)
    carry_in = jnp.where((seg_local == 0)[:, None], jnp.exp(cum_log), 0.0)
    carry_out = jnp.where(
        (seg_local == seg_local[-1])[:, None], jnp.exp(cum_log[-1][None, :] - cum_log), 0.0
    )
    decay_all = jnp.where(seg_local[-1] == 0, jnp.exp(cum_log[-1]), 0.0)
    return (cum_log, seg_local, position, carry_in, carry_out, decay_all)


def weights_of(cum_log, seg_local):
    count = seg_local.shape[0]
    index = jnp.arange(count, dtype=jnp.int32)
    allowed = (seg_local[:, None] == seg_local[None, :]) & (index[:, None] >= index[None, :])
    spread = cum_log.T[:, :, None] - cum_log.T[:, None, :]
    return jnp.where(allowed[None], jnp.exp(jnp.where(allowed[None], spread, 0.0)), 0.0)


def forward_combine(earlier, later):
    return (earlier[0] * later[0], later[0][:, None, None] * earlier[1] + later[1])


def backward_combine(earlier, later):
    return (later[0] * earlier[0], later[1] + later[0][:, None, None] * earlier[1])


def on_device(
    queries, keys, values, output_gradient, document_lengths, cutoff_rows, head_decay_rate
):
    row_count = queries.shape[1]
    query_block = queries.reshape(row_count, HEADS, HEAD_DIM)
    key_block = keys.reshape(row_count, HEADS, HEAD_DIM)
    value_block = values.reshape(row_count, HEADS, HEAD_DIM)
    gradient_block = output_gradient.reshape(row_count, HEADS, HEAD_DIM)
    block_piece = lax.axis_index("seq")
    row_position = block_piece * row_count + jnp.arange(row_count, dtype=jnp.int32)
    length_list = document_lengths[0]
    start_list = jnp.cumsum(length_list) - length_list
    cum_log, seg_local, position, carry_in, carry_out, decay_all = block_mask_list(
        head_decay_rate, cutoff_rows[0], row_position, start_list
    )
    key_f = key_block.astype(jnp.float32)
    value_f = value_block.astype(jnp.float32)
    grad_f = gradient_block.astype(jnp.float32)
    query_f = query_block.astype(jnp.float32)
    state_local = jnp.einsum(
        "the,thf->hef", carry_out[:, :, None] * key_f, value_f, precision=state_mode
    )
    back_local = jnp.einsum(
        "she,shf->hef", carry_in[:, :, None] * query_f, grad_f, precision=state_mode
    )
    identity = (jnp.ones_like(decay_all), jnp.zeros_like(state_local))
    state_input = carried_in((decay_all, state_local), "seq", forward_combine, identity, False)[1]
    backward_input = carried_in((decay_all, back_local), "seq", backward_combine, identity, True)[1]
    weight = weights_of(cum_log, seg_local)
    scores = jnp.einsum("she,the->hst", query_block, key_block, preferred_element_type=jnp.float32)
    grad_scores = jnp.einsum(
        "shf,thf->hst", gradient_block, value_block, preferred_element_type=jnp.float32
    )
    attn_prob = (weight * scores).astype(jnp.bfloat16)
    grad_prob = (weight * grad_scores).astype(jnp.bfloat16)
    value_full = jnp.einsum(
        "hst,shf->thf", attn_prob, gradient_block, preferred_element_type=jnp.float32
    )
    value_full = value_full + carry_out[:, :, None] * jnp.einsum(
        "the,hef->thf", key_f, backward_input, precision=state_mode
    )
    query_full = jnp.einsum(
        "hst,the->she", grad_prob, key_block, preferred_element_type=jnp.float32
    )
    query_full = query_full + carry_in[:, :, None] * jnp.einsum(
        "shf,hef->she", grad_f, state_input, precision=state_mode
    )
    key_full = jnp.einsum(
        "hst,she->the", grad_prob, query_block, preferred_element_type=jnp.float32
    )
    key_full = key_full + carry_out[:, :, None] * jnp.einsum(
        "thf,hef->the", value_f, backward_input, precision=state_mode
    )
    inner_step = jnp.sum(key_f * key_full, axis=2) - jnp.sum(query_f * query_full, axis=2)
    rate_part = jnp.sum(position[:, None] * inner_step, axis=0)
    rate_total = lax.psum(rate_part, ("seq", "dp"))
    token_total = row_count * lax.axis_size("seq") * lax.axis_size("dp")
    rate_grad = head_decay_rate * rate_total / math.sqrt(token_total)
    out_shape = (1, row_count, HEADS * HEAD_DIM)
    return (
        query_full.astype(jnp.bfloat16).reshape(out_shape),
        key_full.astype(jnp.bfloat16).reshape(out_shape),
        value_full.astype(jnp.bfloat16).reshape(out_shape),
        rate_grad,
    )


MESH_ID = pl.DeviceIdType.MESH
CHUNK_HEADS = 2
CHUNKS = HEADS // CHUNK_HEADS
MASKED = -1e30


def dot(a, b, contract):
    return lax.dot_general(
        a, b, ((contract[:1], contract[1:]), ((), ())), preferred_element_type=jnp.float32
    )


def halves(array):
    high = array.astype(jnp.bfloat16)
    return high, (array - high.astype(jnp.float32)).astype(jnp.bfloat16)


def near_kernel(
    lengths_far,
    rates_far,
    cutoffs_far,
    queries_far,
    keys_far,
    values_far,
    gradients_far,
    query_out,
    key_out,
    value_out,
    rate_out,
    lengths,
    rates,
    cutoffs,
    queries,
    keys,
    values,
    gradients,
    spread,
    distance,
    log_in,
    log_out,
    place,
    decays,
    near_decays,
    states,
    from_pair,
    from_line,
    relayed,
    query_sum,
    key_sum,
    value_sum,
    rate_rows,
    rate_dp,
    rate_seq,
    loaded,
    pair_send,
    pair_recv,
    line_send,
    line_recv,
    relay_send,
    relay_recv,
    decay_send,
    decay_recv,
    dp_send,
    dp_recv,
    seq_send,
    seq_recv,
):
    n_seq, n_dp = lax.axis_size("seq"), lax.axis_size("dp")
    block, part = lax.axis_index("seq"), lax.axis_index("dp")
    rows = queries.shape[0]
    side = lax.rem(block, 2)
    pair = block + 1 - 2 * side
    is_first, is_last = block < 2, block >= n_seq - 2
    has_relay = jnp.where(side == 1, block, n_seq - 1 - block) >= 2
    gets_relay = jnp.where(side == 0, block, n_seq - 1 - block) >= 2

    loads = [
        pltpu.make_async_copy(far, near, loaded.at[i])
        for i, (far, near) in enumerate(
            (
                (lengths_far, lengths),
                (cutoffs_far, cutoffs),
                (rates_far, rates),
                (keys_far.at[0], keys),
                (values_far.at[0], values),
                (queries_far.at[0], queries),
                (gradients_far.at[0], gradients),
            )
        )
    ]
    for load in loads:
        load.start()

    barrier = pltpu.get_barrier_semaphore()
    for other in range(1, n_seq):
        pl.semaphore_signal(
            barrier,
            inc=1,
            device_id={"seq": lax.rem(block + other, n_seq)},
            device_id_type=MESH_ID,
        )
    for other in range(1, n_dp):
        pl.semaphore_signal(
            barrier, inc=1, device_id={"dp": lax.rem(part + other, n_dp)}, device_id_type=MESH_ID
        )

    for load in loads[:3]:
        load.wait()

    first = block * rows
    starts, total = [], jnp.int32(0)
    for j in range(lengths.shape[1]):
        starts.append(total)
        total = total + lengths[0, j]

    def segment(local):
        count = jnp.zeros(local.shape, jnp.int32)
        for start in starts:
            count = count + jnp.where((start >= first) & (local + first >= start), 1, 0)
        return count

    row_of = lax.broadcasted_iota(jnp.int32, (rows, rows), 0)
    column_of = lax.broadcasted_iota(jnp.int32, (rows, rows), 1)
    cut_row = cutoffs[...].astype(jnp.float32)
    cut_all = jnp.broadcast_to(cut_row, (rows, rows))
    count_column = jnp.sum(jnp.where(column_of <= row_of, cut_all, 0.0), axis=1, keepdims=True)
    cut_column = jnp.sum(jnp.where(column_of == row_of, cut_all, 0.0), axis=1, keepdims=True)
    count_row = jnp.sum(jnp.where(row_of <= column_of, cut_column, 0.0), axis=0, keepdims=True)
    count_last = jnp.sum(cut_row, axis=1, keepdims=True)
    local = lax.broadcasted_iota(jnp.int32, (rows, HEAD_DIM), 0)
    last = jnp.full((rows, HEAD_DIM), rows - 1, jnp.int32)
    piece = segment(local)
    piece_last = segment(last)
    log_in[...] = jnp.where(piece == 0, count_column * cutoff_logarithm, MASKED)
    log_out[...] = jnp.where(
        piece == piece_last, (count_last - count_column) * cutoff_logarithm, MASKED
    )
    log_all = jnp.where(piece_last[:1] == 0, count_last * cutoff_logarithm, MASKED)
    for h in range(HEADS):
        decays[h : h + 1, :] = jnp.exp(log_all - rates[h] * float(rows))

    @pl.when(is_first)
    def _():
        from_line[0] = jnp.zeros(from_line.shape[1:], jnp.float32)

    @pl.when(is_last)
    def _():
        from_line[1] = jnp.zeros(from_line.shape[1:], jnp.float32)

    @pl.when(block == 0)
    def _():
        near_decays[0] = jnp.zeros(near_decays.shape[1:], jnp.float32)

    @pl.when(block == n_seq - 1)
    def _():
        near_decays[1] = jnp.zeros(near_decays.shape[1:], jnp.float32)

    @pl.when(jnp.logical_not(gets_relay))
    def _():
        relayed[...] = jnp.zeros(relayed.shape, jnp.float32)

    def chunk_of(chunk):
        return pl.ds(pl.multiple_of(chunk * CHUNK_HEADS, CHUNK_HEADS), CHUNK_HEADS)

    def pair_copy(chunk):
        return pltpu.make_async_remote_copy(
            src_ref=states.at[side, chunk_of(chunk)],
            dst_ref=from_pair.at[chunk_of(chunk)],
            send_sem=pair_send.at[chunk],
            recv_sem=pair_recv.at[chunk],
            device_id={"seq": pair},
            device_id_type=MESH_ID,
        )

    def line_copy(way, chunk):
        target = jnp.minimum(block + 2, n_seq - 1) if way == 0 else jnp.maximum(block - 2, 0)
        return pltpu.make_async_remote_copy(
            src_ref=states.at[way, chunk_of(chunk)],
            dst_ref=from_line.at[way, chunk_of(chunk)],
            send_sem=line_send.at[way, chunk],
            recv_sem=line_recv.at[way, chunk],
            device_id={"seq": target},
            device_id_type=MESH_ID,
        )

    def relay_copy(chunk):
        return pltpu.make_async_remote_copy(
            src_ref=from_line.at[1 - side, chunk_of(chunk)],
            dst_ref=relayed.at[chunk_of(chunk)],
            send_sem=relay_send.at[chunk],
            recv_sem=relay_recv.at[chunk],
            device_id={"seq": pair},
            device_id_type=MESH_ID,
        )

    def decay_copy(way):
        target = jnp.minimum(block + 1, n_seq - 1) if way == 0 else jnp.maximum(block - 1, 0)
        return pltpu.make_async_remote_copy(
            src_ref=decays,
            dst_ref=near_decays.at[way],
            send_sem=decay_send.at[way],
            recv_sem=decay_recv.at[way],
            device_id={"seq": target},
            device_id_type=MESH_ID,
        )

    def head_columns(head):
        return pl.ds(pl.multiple_of(head * HEAD_DIM, HEAD_DIM), HEAD_DIM)

    def rows_since():
        return lax.broadcasted_iota(jnp.int32, (rows, HEAD_DIM), 0).astype(jnp.float32)

    def carry_in_of(head):
        return jnp.exp(log_in[...] - rates[head] * (rows_since() + 1.0))

    def carry_out_of(head):
        return jnp.exp(log_out[...] - rates[head] * (float(rows - 1) - rows_since()))

    pl.semaphore_wait(barrier, n_seq - 1 + n_dp - 1)

    not_end = jnp.logical_not(block == n_seq - 1)
    not_begin = jnp.logical_not(block == 0)

    @pl.when(not_end)
    def _():
        decay_copy(0).start()

    @pl.when(not_begin)
    def _():
        decay_copy(1).start()

    def own_states(chunk, carry):
        for inner in range(CHUNK_HEADS):
            head = chunk * CHUNK_HEADS + inner
            at = head_columns(head)
            high, low = halves(carry_out_of(head) * keys[:, at].astype(jnp.float32))
            value = values[:, at]
            states[0, head] = dot(high, value, (0, 0)) + dot(low, value, (0, 0))
            high, low = halves(carry_in_of(head) * queries[:, at].astype(jnp.float32))
            gradient = gradients[:, at]
            states[1, head] = dot(high, gradient, (0, 0)) + dot(low, gradient, (0, 0))
        pair_copy(chunk).start()

        @pl.when(jnp.logical_not(is_last))
        def _():
            line_copy(0, chunk).start()

        @pl.when(jnp.logical_not(is_first))
        def _():
            line_copy(1, chunk).start()

        return carry

    for load in loads[3:]:
        load.wait()
    lax.fori_loop(0, CHUNKS, own_states, 0)

    piece_row = segment(lax.broadcasted_iota(jnp.int32, (1, rows), 1))
    allowed = (piece[:, :1] == piece_row) & (row_of >= column_of)
    spread[...] = jnp.where(allowed, (count_column - count_row) * cutoff_logarithm, MASKED)
    distance[...] = (row_of - column_of).astype(jnp.float32)
    begin = jnp.zeros((rows, HEAD_DIM), jnp.int32)
    for start in starts:
        begin = jnp.maximum(begin, jnp.where(local + first >= start, start, 0))
    place[...] = (local + first - begin).astype(jnp.float32)

    def within(chunk, carry):
        for inner in range(CHUNK_HEADS):
            head = chunk * CHUNK_HEADS + inner
            at = head_columns(head)
            for step, (low, high) in enumerate(((0, rows - HEAD_DIM), (rows - HEAD_DIM, rows))):
                here, upto = slice(low, high), slice(0, high)
                query, key = queries[here, at], keys[upto, at]
                value, gradient = values[upto, at], gradients[here, at]
                weight = jnp.exp(spread[here, upto] - rates[head] * distance[here, upto])
                attn_prob = (weight * dot(query, key, (1, 1))).astype(jnp.bfloat16)
                grad_prob = (weight * dot(gradient, value, (1, 1))).astype(jnp.bfloat16)
                query_sum[here, at] = dot(grad_prob, key, (1, 0))
                value_part = dot(attn_prob, gradient, (0, 0))
                key_part = dot(grad_prob, query, (0, 0))
                if step == 0:
                    value_sum[upto, at] = value_part
                    key_sum[upto, at] = key_part
                else:
                    value_sum[:low, at] += value_part[:low]
                    key_sum[:low, at] += key_part[:low]
                    value_sum[low:, at] = value_part[low:]
                    key_sum[low:, at] = key_part[low:]

        @pl.when(has_relay)
        def _():
            @pl.when(side == 1)
            def _():
                line_copy(0, chunk).wait_recv()

            @pl.when(side == 0)
            def _():
                line_copy(1, chunk).wait_recv()

            relay_copy(chunk).start()

        return carry

    lax.fori_loop(0, CHUNKS, within, 0)

    @pl.when(not_begin)
    def _():
        decay_copy(0).wait_recv()

    @pl.when(not_end)
    def _():
        decay_copy(1).wait_recv()

    def twice(array):
        return jnp.concatenate((array, array), axis=1)

    def across(chunk, carry):
        pair_copy(chunk).wait_recv()

        @pl.when((side == 0) & jnp.logical_not(is_first))
        def _():
            line_copy(0, chunk).wait_recv()

        @pl.when((side == 1) & jnp.logical_not(is_last))
        def _():
            line_copy(1, chunk).wait_recv()

        @pl.when(gets_relay)
        def _():
            relay_copy(chunk).wait_recv()

        for inner in range(CHUNK_HEADS):
            head = chunk * CHUNK_HEADS + inner
            at = head_columns(head)
            paired, passed = from_pair[head], relayed[head]
            before = jnp.where(side == 0, passed, paired)
            after = jnp.where(side == 0, paired, passed)
            state_in = before + near_decays[0, pl.ds(head, 1), :] * from_line[0, head]
            grad_in = after + near_decays[1, pl.ds(head, 1), :] * from_line[1, head]
            state_in = jnp.concatenate(halves(state_in), axis=1)
            high, low = halves(grad_in)
            grad_wide = jnp.concatenate((high, low), axis=1)
            grad_tall = jnp.concatenate((high, low), axis=0)
            query, key = queries[:, at], keys[:, at]
            carry_in, carry_out = carry_in_of(head), carry_out_of(head)
            query_full = query_sum[:, at] + carry_in * dot(
                twice(gradients[:, at]), state_in, (1, 1)
            )
            key_full = key_sum[:, at] + carry_out * dot(twice(values[:, at]), grad_wide, (1, 1))
            value_full = value_sum[:, at] + carry_out * dot(twice(key), grad_tall, (1, 0))
            query_out[:, at] = query_full.astype(jnp.bfloat16)
            key_out[:, at] = key_full.astype(jnp.bfloat16)
            value_out[:, at] = value_full.astype(jnp.bfloat16)
            inner_step = key.astype(jnp.float32) * key_full - query.astype(jnp.float32) * query_full
            rate_rows[pl.ds(head, 1), :] = jnp.sum(
                place[...] * inner_step, axis=0, keepdims=True
            )
        return carry

    lax.fori_loop(0, CHUNKS, across, 0)

    def dp_copy(other):
        return pltpu.make_async_remote_copy(
            src_ref=rate_rows,
            dst_ref=rate_dp.at[other],
            send_sem=dp_send.at[other],
            recv_sem=dp_recv.at[other],
            device_id={"dp": lax.rem(part + other, n_dp)},
            device_id_type=MESH_ID,
        )

    def seq_copy(other):
        return pltpu.make_async_remote_copy(
            src_ref=rate_seq.at[0],
            dst_ref=rate_seq.at[other],
            send_sem=seq_send.at[other],
            recv_sem=seq_recv.at[other],
            device_id={"seq": lax.rem(block + other, n_seq)},
            device_id_type=MESH_ID,
        )

    for other in range(1, n_dp):
        dp_copy(other).start()
    summed = rate_rows[...]
    for other in range(1, n_dp):
        dp_copy(other).wait_recv()
        summed = summed + rate_dp[other]
    rate_seq[0] = summed
    for other in range(1, n_seq):
        seq_copy(other).start()
    for other in range(1, n_seq):
        seq_copy(other).wait_recv()
        summed = summed + rate_seq[other]
    scale = 1.0 / math.sqrt(rows * n_seq * n_dp)
    lane = lax.broadcasted_iota(jnp.int32, (1, HEAD_DIM), 1)
    summed = jnp.sum(summed, axis=1, keepdims=True) * scale
    result = jnp.zeros((1, HEAD_DIM), jnp.float32)
    for h in range(HEADS):
        result = jnp.where(lane == h, rates[h] * summed[h : h + 1], result)
    rate_out[...] = result[:, :HEADS]

    for other in range(1, n_dp):
        dp_copy(other).wait_send()
    for other in range(1, n_seq):
        seq_copy(other).wait_send()

    @pl.when(not_end)
    def _():
        decay_copy(0).wait_send()

    @pl.when(not_begin)
    def _():
        decay_copy(1).wait_send()

    def sent(chunk, carry):
        pair_copy(chunk).wait_send()

        @pl.when(jnp.logical_not(is_last))
        def _():
            line_copy(0, chunk).wait_send()

        @pl.when(jnp.logical_not(is_first))
        def _():
            line_copy(1, chunk).wait_send()

        @pl.when(has_relay)
        def _():
            relay_copy(chunk).wait_send()

        return carry

    lax.fori_loop(0, CHUNKS, sent, 0)


def finish_kernel(*refs):
    count = (len(refs) - 1) // 2
    copies = [
        pltpu.make_async_copy(refs[i], refs[count + i], refs[-1].at[i]) for i in range(count)
    ]
    for copy in copies:
        copy.start()
    for copy in copies:
        copy.wait()


def on_device_near(
    queries, keys, values, output_gradient, document_lengths, cutoff_rows, head_decay_rate
):
    rows, width = queries.shape[1:]
    n_seq, n_dp = lax.axis_size("seq"), lax.axis_size("dp")
    vmem = pl.BlockSpec(memory_space=pltpu.VMEM)
    hbm = pl.BlockSpec(memory_space=pltpu.HBM)
    anywhere = pl.BlockSpec(memory_space=pl.ANY)
    out = jax.ShapeDtypeStruct((rows, width), jnp.bfloat16)
    state = (HEADS, HEAD_DIM, HEAD_DIM)
    dma = pltpu.SemaphoreType.DMA
    near = pltpu.VMEM((rows, width), jnp.bfloat16)
    results = pl.pallas_call(
        near_kernel,
        out_shape=(out, out, out, jax.ShapeDtypeStruct((1, HEADS), jnp.float32)),
        in_specs=[hbm] * 7,
        out_specs=[vmem] * 4,
        scratch_shapes=[
            pltpu.SMEM(document_lengths.shape, jnp.int32),
            pltpu.SMEM(head_decay_rate.shape, jnp.float32),
            pltpu.VMEM(cutoff_rows.shape, jnp.int32),
            near,
            near,
            near,
            near,
            pltpu.VMEM((rows, rows), jnp.float32),
            pltpu.VMEM((rows, rows), jnp.float32),
            pltpu.VMEM((rows, HEAD_DIM), jnp.float32),
            pltpu.VMEM((rows, HEAD_DIM), jnp.float32),
            pltpu.VMEM((rows, HEAD_DIM), jnp.float32),
            pltpu.VMEM((HEADS, HEAD_DIM), jnp.float32),
            pltpu.VMEM((2, HEADS, HEAD_DIM), jnp.float32),
            pltpu.VMEM((2,) + state, jnp.float32),
            pltpu.VMEM(state, jnp.float32),
            pltpu.VMEM((2,) + state, jnp.float32),
            pltpu.VMEM(state, jnp.float32),
            pltpu.VMEM((rows, width), jnp.float32),
            pltpu.VMEM((rows, width), jnp.float32),
            pltpu.VMEM((rows, width), jnp.float32),
            pltpu.VMEM((HEADS, HEAD_DIM), jnp.float32),
            pltpu.VMEM((n_dp, HEADS, HEAD_DIM), jnp.float32),
            pltpu.VMEM((n_seq, HEADS, HEAD_DIM), jnp.float32),
            dma((7,)),
            dma((CHUNKS,)),
            dma((CHUNKS,)),
            dma((2, CHUNKS)),
            dma((2, CHUNKS)),
            dma((CHUNKS,)),
            dma((CHUNKS,)),
            dma((2,)),
            dma((2,)),
            dma((n_dp,)),
            dma((n_dp,)),
            dma((n_seq,)),
            dma((n_seq,)),
        ],
        compiler_params=pltpu.CompilerParams(
            collective_id=0, has_side_effects=True, vmem_limit_bytes=48 * 1024 * 1024
        ),
    )(
        document_lengths,
        head_decay_rate,
        cutoff_rows,
        queries,
        keys,
        values,
        output_gradient,
    )
    query_grad, key_grad, value_grad, rate_grad = pl.pallas_call(
        finish_kernel,
        out_shape=tuple(jax.ShapeDtypeStruct(a.shape, a.dtype) for a in results),
        in_specs=[vmem] * 4,
        out_specs=[anywhere] * 4,
        scratch_shapes=[dma((4,))],
    )(*results)
    return (query_grad[None], key_grad[None], value_grad[None], rate_grad[0])


def solution(mesh):
    in_specs = (
        P("dp", "seq", None),
        P("dp", "seq", None),
        P("dp", "seq", None),
        P("dp", "seq", None),
        P("dp", None),
        P("dp", "seq"),
        P(),
    )
    out_specs = (P("dp", "seq", None), P("dp", "seq", None), P("dp", "seq", None), P())
    near = mesh.shape["seq"] == 8
    return jax.shard_map(
        on_device_near if near else on_device, mesh=mesh, in_specs=in_specs, out_specs=out_specs, check_vma=False
    )
```

```python
import functools
import math

import jax
import jax.numpy as jnp
from jax import lax
from jax.experimental import pallas as pl
from jax.experimental.pallas import tpu as pltpu
from jax.sharding import PartitionSpec as P

HEADS = 16
HEAD_DIM = 128


cutoff_logarithm = math.log(0.7)
state_mode = lax.Precision.HIGH


def carried_in(part, axis, combine, identity, reverse):
    count = lax.axis_size(axis)
    place = lax.axis_index(axis)
    ahead = count - 1 - place if reverse else place
    gathered = jax.tree.map(lambda a: lax.all_gather(a, axis), part)
    state = jax.tree.map(lambda a, e: jnp.zeros_like(a) + jnp.asarray(e, a.dtype), part, identity)

    def one(step, state):
        source = count - 1 - step if reverse else step
        return combine(
            state, jax.tree.map(lambda a: lax.dynamic_index_in_dim(a, source, 0, False), gathered)
        )

    return lax.fori_loop(0, ahead, one, state)


def block_mask_list(head_decay_rate, cutoff_list, row_position, start_list):
    is_start = jnp.any(row_position[:, None] == start_list[None, :], axis=1)
    seg_local = jnp.cumsum(is_start.astype(jnp.int32))
    begin = jnp.max(
        jnp.where(start_list[None, :] <= row_position[:, None], start_list[None, :], 0), axis=1
    )
    position = (row_position - begin).astype(jnp.float32)
    logarithm_step = (
        cutoff_list.astype(jnp.float32)[:, None] * cutoff_logarithm - head_decay_rate[None, :]
    )
    cum_log = jnp.cumsum(logarithm_step, axis=0)
    carry_in = jnp.where((seg_local == 0)[:, None], jnp.exp(cum_log), 0.0)
    carry_out = jnp.where(
        (seg_local == seg_local[-1])[:, None], jnp.exp(cum_log[-1][None, :] - cum_log), 0.0
    )
    decay_all = jnp.where(seg_local[-1] == 0, jnp.exp(cum_log[-1]), 0.0)
    return (cum_log, seg_local, position, carry_in, carry_out, decay_all)


def weights_of(cum_log, seg_local):
    count = seg_local.shape[0]
    index = jnp.arange(count, dtype=jnp.int32)
    allowed = (seg_local[:, None] == seg_local[None, :]) & (index[:, None] >= index[None, :])
    spread = cum_log.T[:, :, None] - cum_log.T[:, None, :]
    return jnp.where(allowed[None], jnp.exp(jnp.where(allowed[None], spread, 0.0)), 0.0)


def forward_combine(earlier, later):
    return (earlier[0] * later[0], later[0][:, None, None] * earlier[1] + later[1])


def backward_combine(earlier, later):
    return (later[0] * earlier[0], later[1] + later[0][:, None, None] * earlier[1])


def on_device(
    queries, keys, values, output_gradient, document_lengths, cutoff_rows, head_decay_rate
):
    row_count = queries.shape[1]
    query_block = queries.reshape(row_count, HEADS, HEAD_DIM)
    key_block = keys.reshape(row_count, HEADS, HEAD_DIM)
    value_block = values.reshape(row_count, HEADS, HEAD_DIM)
    gradient_block = output_gradient.reshape(row_count, HEADS, HEAD_DIM)
    block_piece = lax.axis_index("seq")
    row_position = block_piece * row_count + jnp.arange(row_count, dtype=jnp.int32)
    length_list = document_lengths[0]
    start_list = jnp.cumsum(length_list) - length_list
    cum_log, seg_local, position, carry_in, carry_out, decay_all = block_mask_list(
        head_decay_rate, cutoff_rows[0], row_position, start_list
    )
    key_f = key_block.astype(jnp.float32)
    value_f = value_block.astype(jnp.float32)
    grad_f = gradient_block.astype(jnp.float32)
    query_f = query_block.astype(jnp.float32)
    state_local = jnp.einsum(
        "the,thf->hef", carry_out[:, :, None] * key_f, value_f, precision=state_mode
    )
    back_local = jnp.einsum(
        "she,shf->hef", carry_in[:, :, None] * query_f, grad_f, precision=state_mode
    )
    identity = (jnp.ones_like(decay_all), jnp.zeros_like(state_local))
    state_input = carried_in((decay_all, state_local), "seq", forward_combine, identity, False)[1]
    backward_input = carried_in((decay_all, back_local), "seq", backward_combine, identity, True)[1]
    weight = weights_of(cum_log, seg_local)
    scores = jnp.einsum("she,the->hst", query_block, key_block, preferred_element_type=jnp.float32)
    grad_scores = jnp.einsum(
        "shf,thf->hst", gradient_block, value_block, preferred_element_type=jnp.float32
    )
    attn_prob = (weight * scores).astype(jnp.bfloat16)
    grad_prob = (weight * grad_scores).astype(jnp.bfloat16)
    value_full = jnp.einsum(
        "hst,shf->thf", attn_prob, gradient_block, preferred_element_type=jnp.float32
    )
    value_full = value_full + carry_out[:, :, None] * jnp.einsum(
        "the,hef->thf", key_f, backward_input, precision=state_mode
    )
    query_full = jnp.einsum(
        "hst,the->she", grad_prob, key_block, preferred_element_type=jnp.float32
    )
    query_full = query_full + carry_in[:, :, None] * jnp.einsum(
        "shf,hef->she", grad_f, state_input, precision=state_mode
    )
    key_full = jnp.einsum(
        "hst,she->the", grad_prob, query_block, preferred_element_type=jnp.float32
    )
    key_full = key_full + carry_out[:, :, None] * jnp.einsum(
        "thf,hef->the", value_f, backward_input, precision=state_mode
    )
    inner_step = jnp.sum(key_f * key_full, axis=2) - jnp.sum(query_f * query_full, axis=2)
    rate_part = jnp.sum(position[:, None] * inner_step, axis=0)
    rate_total = lax.psum(rate_part, ("seq", "dp"))
    token_total = row_count * lax.axis_size("seq") * lax.axis_size("dp")
    rate_grad = head_decay_rate * rate_total / math.sqrt(token_total)
    out_shape = (1, row_count, HEADS * HEAD_DIM)
    return (
        query_full.astype(jnp.bfloat16).reshape(out_shape),
        key_full.astype(jnp.bfloat16).reshape(out_shape),
        value_full.astype(jnp.bfloat16).reshape(out_shape),
        rate_grad,
    )


MESH_ID = pl.DeviceIdType.MESH
CHUNK_HEADS = 2
CHUNKS = HEADS // CHUNK_HEADS
MASKED = -1e30


def dot(a, b, contract):
    return lax.dot_general(
        a, b, ((contract[:1], contract[1:]), ((), ())), preferred_element_type=jnp.float32
    )


def halves(array):
    high = array.astype(jnp.bfloat16)
    return high, (array - high.astype(jnp.float32)).astype(jnp.bfloat16)


def near_kernel(
    lengths_far,
    rates_far,
    cutoffs_far,
    queries_far,
    keys_far,
    values_far,
    gradients_far,
    query_out,
    key_out,
    value_out,
    rate_out,
    lengths,
    rates,
    cutoffs,
    queries,
    keys,
    values,
    gradients,
    spread,
    distance,
    log_in,
    log_out,
    place,
    decays,
    near_decays,
    states,
    from_pair,
    from_line,
    relayed,
    query_sum,
    key_sum,
    value_sum,
    rate_rows,
    rate_dp,
    rate_seq,
    loaded,
    pair_send,
    pair_recv,
    line_send,
    line_recv,
    relay_send,
    relay_recv,
    direct_send,
    decay_send,
    decay_recv,
    dp_send,
    dp_recv,
    seq_send,
    seq_recv,
):
    n_seq, n_dp = lax.axis_size("seq"), lax.axis_size("dp")
    block, part = lax.axis_index("seq"), lax.axis_index("dp")
    rows = queries.shape[0]
    side = lax.rem(block, 2)
    pair = block + 1 - 2 * side
    is_first, is_last = block < 2, block >= n_seq - 2
    has_relay = jnp.where(side == 1, block, n_seq - 1 - block) >= 2
    gets_relay = jnp.where(side == 0, block, n_seq - 1 - block) >= 2

    line, n_line = block // 2, n_seq // 2
    own_direct = jnp.where(side == 1, n_line - 1 - line, line) * CHUNKS // n_line
    past_direct = jnp.where(side == 1, n_line - line, line + 1) * CHUNKS // n_line

    def directs(chunk):
        return chunk >= CHUNKS - own_direct

    def relays(chunk):
        return has_relay & (chunk < CHUNKS - past_direct)

    loads = [
        pltpu.make_async_copy(far, near, loaded.at[i])
        for i, (far, near) in enumerate(
            (
                (lengths_far, lengths),
                (cutoffs_far, cutoffs),
                (rates_far, rates),
                (keys_far.at[0], keys),
                (values_far.at[0], values),
                (queries_far.at[0], queries),
                (gradients_far.at[0], gradients),
            )
        )
    ]
    for load in loads:
        load.start()

    barrier = pltpu.get_barrier_semaphore()
    for other in range(1, n_seq):
        pl.semaphore_signal(
            barrier,
            inc=1,
            device_id={"seq": lax.rem(block + other, n_seq)},
            device_id_type=MESH_ID,
        )
    for other in range(1, n_dp):
        pl.semaphore_signal(
            barrier, inc=1, device_id={"dp": lax.rem(part + other, n_dp)}, device_id_type=MESH_ID
        )

    for load in loads[:3]:
        load.wait()

    first = block * rows
    starts, total = [], jnp.int32(0)
    for j in range(lengths.shape[1]):
        starts.append(total)
        total = total + lengths[0, j]

    def segment(local):
        count = jnp.zeros(local.shape, jnp.int32)
        for start in starts:
            count = count + jnp.where((start >= first) & (local + first >= start), 1, 0)
        return count

    row_of = lax.broadcasted_iota(jnp.int32, (rows, rows), 0)
    column_of = lax.broadcasted_iota(jnp.int32, (rows, rows), 1)
    cut_row = cutoffs[...].astype(jnp.float32)
    cut_all = jnp.broadcast_to(cut_row, (rows, rows))
    count_column = jnp.sum(jnp.where(column_of <= row_of, cut_all, 0.0), axis=1, keepdims=True)
    cut_column = jnp.sum(jnp.where(column_of == row_of, cut_all, 0.0), axis=1, keepdims=True)
    count_row = jnp.sum(jnp.where(row_of <= column_of, cut_column, 0.0), axis=0, keepdims=True)
    count_last = jnp.sum(cut_row, axis=1, keepdims=True)
    local = lax.broadcasted_iota(jnp.int32, (rows, HEAD_DIM), 0)
    last = jnp.full((rows, HEAD_DIM), rows - 1, jnp.int32)
    piece = segment(local)
    piece_last = segment(last)
    log_in[...] = jnp.where(piece == 0, count_column * cutoff_logarithm, MASKED)
    log_out[...] = jnp.where(
        piece == piece_last, (count_last - count_column) * cutoff_logarithm, MASKED
    )
    log_all = jnp.where(piece_last[:1] == 0, count_last * cutoff_logarithm, MASKED)
    for h in range(HEADS):
        decays[h : h + 1, :] = jnp.exp(log_all - rates[h] * float(rows))

    @pl.when(is_first)
    def _():
        from_line[0] = jnp.zeros(from_line.shape[1:], jnp.float32)

    @pl.when(is_last)
    def _():
        from_line[1] = jnp.zeros(from_line.shape[1:], jnp.float32)

    @pl.when(block == 0)
    def _():
        near_decays[0] = jnp.zeros(near_decays.shape[1:], jnp.float32)

    @pl.when(block == n_seq - 1)
    def _():
        near_decays[1] = jnp.zeros(near_decays.shape[1:], jnp.float32)

    @pl.when(jnp.logical_not(gets_relay))
    def _():
        relayed[...] = jnp.zeros(relayed.shape, jnp.float32)

    def chunk_of(chunk):
        return pl.ds(pl.multiple_of(chunk * CHUNK_HEADS, CHUNK_HEADS), CHUNK_HEADS)

    def pair_copy(chunk):
        return pltpu.make_async_remote_copy(
            src_ref=states.at[side, chunk_of(chunk)],
            dst_ref=from_pair.at[chunk_of(chunk)],
            send_sem=pair_send.at[chunk],
            recv_sem=pair_recv.at[chunk],
            device_id={"seq": pair},
            device_id_type=MESH_ID,
        )

    def line_copy(way, chunk):
        target = jnp.minimum(block + 2, n_seq - 1) if way == 0 else jnp.maximum(block - 2, 0)
        return pltpu.make_async_remote_copy(
            src_ref=states.at[way, chunk_of(chunk)],
            dst_ref=from_line.at[way, chunk_of(chunk)],
            send_sem=line_send.at[way, chunk],
            recv_sem=line_recv.at[way, chunk],
            device_id={"seq": target},
            device_id_type=MESH_ID,
        )

    def relay_copy(chunk):
        return pltpu.make_async_remote_copy(
            src_ref=from_line.at[1 - side, chunk_of(chunk)],
            dst_ref=relayed.at[chunk_of(chunk)],
            send_sem=relay_send.at[chunk],
            recv_sem=relay_recv.at[chunk],
            device_id={"seq": pair},
            device_id_type=MESH_ID,
        )

    def direct_copy(chunk):
        return pltpu.make_async_remote_copy(
            src_ref=states.at[1 - side, chunk_of(chunk)],
            dst_ref=relayed.at[chunk_of(chunk)],
            send_sem=direct_send.at[chunk],
            recv_sem=relay_recv.at[chunk],
            device_id={
                "seq": jnp.clip(block - 1 + 2 * side, 0, n_seq - 1),
            },
            device_id_type=MESH_ID,
        )

    def decay_copy(way):
        target = jnp.minimum(block + 1, n_seq - 1) if way == 0 else jnp.maximum(block - 1, 0)
        return pltpu.make_async_remote_copy(
            src_ref=decays,
            dst_ref=near_decays.at[way],
            send_sem=decay_send.at[way],
            recv_sem=decay_recv.at[way],
            device_id={"seq": target},
            device_id_type=MESH_ID,
        )

    def head_columns(head):
        return pl.ds(pl.multiple_of(head * HEAD_DIM, HEAD_DIM), HEAD_DIM)

    def rows_since():
        return lax.broadcasted_iota(jnp.int32, (rows, HEAD_DIM), 0).astype(jnp.float32)

    def carry_in_of(head):
        return jnp.exp(log_in[...] - rates[head] * (rows_since() + 1.0))

    def carry_out_of(head):
        return jnp.exp(log_out[...] - rates[head] * (float(rows - 1) - rows_since()))

    pl.semaphore_wait(barrier, n_seq - 1 + n_dp - 1)

    not_end = jnp.logical_not(block == n_seq - 1)
    not_begin = jnp.logical_not(block == 0)

    @pl.when(not_end)
    def _():
        decay_copy(0).start()

    @pl.when(not_begin)
    def _():
        decay_copy(1).start()

    def own_states(chunk, carry):
        for inner in range(CHUNK_HEADS):
            head = chunk * CHUNK_HEADS + inner
            at = head_columns(head)
            high, low = halves(carry_out_of(head) * keys[:, at].astype(jnp.float32))
            value = values[:, at]
            states[0, head] = dot(high, value, (0, 0)) + dot(low, value, (0, 0))
            high, low = halves(carry_in_of(head) * queries[:, at].astype(jnp.float32))
            gradient = gradients[:, at]
            states[1, head] = dot(high, gradient, (0, 0)) + dot(low, gradient, (0, 0))
        pair_copy(chunk).start()

        @pl.when(jnp.logical_not(is_last))
        def _():
            line_copy(0, chunk).start()

        @pl.when(jnp.logical_not(is_first))
        def _():
            line_copy(1, chunk).start()

        @pl.when(directs(chunk))
        def _():
            direct_copy(chunk).start()

        return carry

    for load in loads[3:]:
        load.wait()
    lax.fori_loop(0, CHUNKS, own_states, 0)

    piece_row = segment(lax.broadcasted_iota(jnp.int32, (1, rows), 1))
    allowed = (piece[:, :1] == piece_row) & (row_of >= column_of)
    spread[...] = jnp.where(allowed, (count_column - count_row) * cutoff_logarithm, MASKED)
    distance[...] = (row_of - column_of).astype(jnp.float32)
    begin = jnp.zeros((rows, HEAD_DIM), jnp.int32)
    for start in starts:
        begin = jnp.maximum(begin, jnp.where(local + first >= start, start, 0))
    place[...] = (local + first - begin).astype(jnp.float32)

    def within(chunk, carry):
        for inner in range(CHUNK_HEADS):
            head = chunk * CHUNK_HEADS + inner
            at = head_columns(head)
            for step, (low, high) in enumerate(((0, rows - HEAD_DIM), (rows - HEAD_DIM, rows))):
                here, upto = slice(low, high), slice(0, high)
                query, key = queries[here, at], keys[upto, at]
                value, gradient = values[upto, at], gradients[here, at]
                weight = jnp.exp(spread[here, upto] - rates[head] * distance[here, upto])
                attn_prob = (weight * dot(query, key, (1, 1))).astype(jnp.bfloat16)
                grad_prob = (weight * dot(gradient, value, (1, 1))).astype(jnp.bfloat16)
                query_sum[here, at] = dot(grad_prob, key, (1, 0))
                value_part = dot(attn_prob, gradient, (0, 0))
                key_part = dot(grad_prob, query, (0, 0))
                if step == 0:
                    value_sum[upto, at] = value_part
                    key_sum[upto, at] = key_part
                else:
                    value_sum[:low, at] += value_part[:low]
                    key_sum[:low, at] += key_part[:low]
                    value_sum[low:, at] = value_part[low:]
                    key_sum[low:, at] = key_part[low:]

        @pl.when(relays(chunk))
        def _():
            @pl.when(side == 1)
            def _():
                line_copy(0, chunk).wait_recv()

            @pl.when(side == 0)
            def _():
                line_copy(1, chunk).wait_recv()

            relay_copy(chunk).start()

        return carry

    lax.fori_loop(0, CHUNKS, within, 0)

    @pl.when(not_begin)
    def _():
        decay_copy(0).wait_recv()

    @pl.when(not_end)
    def _():
        decay_copy(1).wait_recv()

    def twice(array):
        return jnp.concatenate((array, array), axis=1)

    def across(chunk, carry):
        pair_copy(chunk).wait_recv()

        @pl.when(jnp.logical_not(is_first | ((side == 1) & relays(chunk))))
        def _():
            line_copy(0, chunk).wait_recv()

        @pl.when(jnp.logical_not(is_last | ((side == 0) & relays(chunk))))
        def _():
            line_copy(1, chunk).wait_recv()

        @pl.when(gets_relay)
        def _():
            relay_copy(chunk).wait_recv()

        for inner in range(CHUNK_HEADS):
            head = chunk * CHUNK_HEADS + inner
            at = head_columns(head)
            paired, passed = from_pair[head], relayed[head]
            before = jnp.where(side == 0, passed, paired)
            after = jnp.where(side == 0, paired, passed)
            state_in = before + near_decays[0, pl.ds(head, 1), :] * from_line[0, head]
            grad_in = after + near_decays[1, pl.ds(head, 1), :] * from_line[1, head]
            state_in = jnp.concatenate(halves(state_in), axis=1)
            high, low = halves(grad_in)
            grad_wide = jnp.concatenate((high, low), axis=1)
            grad_tall = jnp.concatenate((high, low), axis=0)
            query, key = queries[:, at], keys[:, at]
            carry_in, carry_out = carry_in_of(head), carry_out_of(head)
            query_full = query_sum[:, at] + carry_in * dot(
                twice(gradients[:, at]), state_in, (1, 1)
            )
            key_full = key_sum[:, at] + carry_out * dot(twice(values[:, at]), grad_wide, (1, 1))
            value_full = value_sum[:, at] + carry_out * dot(twice(key), grad_tall, (1, 0))
            query_out[:, at] = query_full.astype(jnp.bfloat16)
            key_out[:, at] = key_full.astype(jnp.bfloat16)
            value_out[:, at] = value_full.astype(jnp.bfloat16)
            inner_step = key.astype(jnp.float32) * key_full - query.astype(jnp.float32) * query_full
            rate_rows[pl.ds(head, 1), :] = jnp.sum(
                place[...] * inner_step, axis=0, keepdims=True
            )
        return carry

    lax.fori_loop(0, CHUNKS, across, 0)

    def dp_copy(other):
        return pltpu.make_async_remote_copy(
            src_ref=rate_rows,
            dst_ref=rate_dp.at[other],
            send_sem=dp_send.at[other],
            recv_sem=dp_recv.at[other],
            device_id={"dp": lax.rem(part + other, n_dp)},
            device_id_type=MESH_ID,
        )

    def seq_copy(other):
        return pltpu.make_async_remote_copy(
            src_ref=rate_seq.at[0],
            dst_ref=rate_seq.at[other],
            send_sem=seq_send.at[other],
            recv_sem=seq_recv.at[other],
            device_id={"seq": lax.rem(block + other, n_seq)},
            device_id_type=MESH_ID,
        )

    for other in range(1, n_dp):
        dp_copy(other).start()
    summed = rate_rows[...]
    for other in range(1, n_dp):
        dp_copy(other).wait_recv()
        summed = summed + rate_dp[other]
    rate_seq[0] = summed
    for other in range(1, n_seq):
        seq_copy(other).start()
    for other in range(1, n_seq):
        seq_copy(other).wait_recv()
        summed = summed + rate_seq[other]
    scale = 1.0 / math.sqrt(rows * n_seq * n_dp)
    lane = lax.broadcasted_iota(jnp.int32, (1, HEAD_DIM), 1)
    summed = jnp.sum(summed, axis=1, keepdims=True) * scale
    result = jnp.zeros((1, HEAD_DIM), jnp.float32)
    for h in range(HEADS):
        result = jnp.where(lane == h, rates[h] * summed[h : h + 1], result)
    rate_out[...] = result[:, :HEADS]

    for other in range(1, n_dp):
        dp_copy(other).wait_send()
    for other in range(1, n_seq):
        seq_copy(other).wait_send()

    @pl.when(not_end)
    def _():
        decay_copy(0).wait_send()

    @pl.when(not_begin)
    def _():
        decay_copy(1).wait_send()

    def sent(chunk, carry):
        pair_copy(chunk).wait_send()

        @pl.when(jnp.logical_not(is_last))
        def _():
            line_copy(0, chunk).wait_send()

        @pl.when(jnp.logical_not(is_first))
        def _():
            line_copy(1, chunk).wait_send()

        @pl.when(relays(chunk))
        def _():
            relay_copy(chunk).wait_send()

        @pl.when(directs(chunk))
        def _():
            direct_copy(chunk).wait_send()

        return carry

    lax.fori_loop(0, CHUNKS, sent, 0)


def on_device_near(
    queries, keys, values, output_gradient, document_lengths, cutoff_rows, head_decay_rate
):
    rows, width = queries.shape[1:]
    n_seq, n_dp = lax.axis_size("seq"), lax.axis_size("dp")
    vmem = pl.BlockSpec(memory_space=pltpu.VMEM)
    hbm = pl.BlockSpec(memory_space=pltpu.HBM)
    out = jax.ShapeDtypeStruct((rows, width), jnp.bfloat16)
    state = (HEADS, HEAD_DIM, HEAD_DIM)
    dma = pltpu.SemaphoreType.DMA
    near = pltpu.VMEM((rows, width), jnp.bfloat16)
    query_grad, key_grad, value_grad, rate_grad = pl.pallas_call(
        near_kernel,
        out_shape=(out, out, out, jax.ShapeDtypeStruct((1, HEADS), jnp.float32)),
        in_specs=[hbm] * 7,
        out_specs=[vmem] * 4,
        scratch_shapes=[
            pltpu.SMEM(document_lengths.shape, jnp.int32),
            pltpu.SMEM(head_decay_rate.shape, jnp.float32),
            pltpu.VMEM(cutoff_rows.shape, jnp.int32),
            near,
            near,
            near,
            near,
            pltpu.VMEM((rows, rows), jnp.float32),
            pltpu.VMEM((rows, rows), jnp.float32),
            pltpu.VMEM((rows, HEAD_DIM), jnp.float32),
            pltpu.VMEM((rows, HEAD_DIM), jnp.float32),
            pltpu.VMEM((rows, HEAD_DIM), jnp.float32),
            pltpu.VMEM((HEADS, HEAD_DIM), jnp.float32),
            pltpu.VMEM((2, HEADS, HEAD_DIM), jnp.float32),
            pltpu.VMEM((2,) + state, jnp.float32),
            pltpu.VMEM(state, jnp.float32),
            pltpu.VMEM((2,) + state, jnp.float32),
            pltpu.VMEM(state, jnp.float32),
            pltpu.VMEM((rows, width), jnp.float32),
            pltpu.VMEM((rows, width), jnp.float32),
            pltpu.VMEM((rows, width), jnp.float32),
            pltpu.VMEM((HEADS, HEAD_DIM), jnp.float32),
            pltpu.VMEM((n_dp, HEADS, HEAD_DIM), jnp.float32),
            pltpu.VMEM((n_seq, HEADS, HEAD_DIM), jnp.float32),
            dma((7,)),
            dma((CHUNKS,)),
            dma((CHUNKS,)),
            dma((2, CHUNKS)),
            dma((2, CHUNKS)),
            dma((CHUNKS,)),
            dma((CHUNKS,)),
            dma((CHUNKS,)),
            dma((2,)),
            dma((2,)),
            dma((n_dp,)),
            dma((n_dp,)),
            dma((n_seq,)),
            dma((n_seq,)),
        ],
        compiler_params=pltpu.CompilerParams(
            collective_id=0, has_side_effects=True, vmem_limit_bytes=48 * 1024 * 1024
        ),
    )(
        document_lengths,
        head_decay_rate,
        cutoff_rows,
        queries,
        keys,
        values,
        output_gradient,
    )
    return (query_grad[None], key_grad[None], value_grad[None], rate_grad[0])


def solution(mesh):
    in_specs = (
        P("dp", "seq", None),
        P("dp", "seq", None),
        P("dp", "seq", None),
        P("dp", "seq", None),
        P("dp", None),
        P("dp", "seq"),
        P(),
    )
    out_specs = (P("dp", "seq", None), P("dp", "seq", None), P("dp", "seq", None), P())
    near = mesh.shape["seq"] == 8
    return jax.shard_map(
        on_device_near if near else on_device, mesh=mesh, in_specs=in_specs, out_specs=out_specs, check_vma=False
    )
```
